32 devices in a mesh: dx: 4 (over z), dy: 8 (over y, x, core).
Axes of the slice: x: 2, y: 2, z: 4, core: 2. Of those that a mesh axis runs over, the one named last changes fastest.
Arguments:
- orbitals: bfloat16 [32, 64, 4096], P(('dx', 'dy')), may hold values from -6 to 6
- offsets: int32 [32, 3], replicated, may hold values from 0 to 31
- pair_list: int32 [256, 2], P(('dx', 'dy')), may hold values from 0 to 31, as said below
- pair_mask: int32 [256], P(('dx', 'dy')), may hold values from 0 to 1, as said below
Outputs:
- exchange: float32 [32, 64, 4096], P(('dx', 'dy'))
The draws below stay inside these ranges and needn't reach their ends.
Inputs may be any that keep to these rules, and one draw needn't show every extreme that they name: `pair_list`: in each spatial domain's block of 8 slots (domain index dx * 8 + dy owns orbitals 1 * that index onward), the first orbital belongs to that domain and the second to it or to one of the eight domains whose x and y domain indices differ by at most one, wrapping around. `pair_mask`: every domain uses at least one slot; in every draw some domain uses all 8.
All inputs are finite; a program needn't handle non-finite values.
Results may differ from the reference program's by a relative error of at most 0.0003.
Values may be sent and summed in bfloat16 or wider, within the bound.
A program may use at most 64 MiB of HBM per device.

```python
import math
import jax
import jax.numpy as jnp
from jax import lax

BOX = 64
ORB_DEV = 1
PAIR_DEV = 8
DOM_X = 4
DOM_Y = 8
ORBS = 32


def draw_orbitals(key, part):
    key = jax.random.fold_in(key, 5)
    keys = jax.random.split(key, 4)
    waves = 4
    amplitude = 0.64
    lowest = BOX * 5 // 32
    highest = BOX * 15 // 32 + 1
    magnitude = jax.random.randint(keys[0], (waves, ORBS, 3), lowest, highest)
    signs = 2 * jax.random.randint(keys[1], (waves, ORBS, 3), 0, 2) - 1
    modes = (magnitude * signs).astype(jnp.int32)
    phases = jax.random.uniform(keys[2], (waves, ORBS), jnp.float32, -math.pi, math.pi)
    cell_x = jnp.arange(BOX, dtype=jnp.int32)
    flat_index = jnp.arange(BOX * BOX, dtype=jnp.int32)
    cell_y = flat_index // BOX
    cell_z = flat_index % BOX
    noise = 0.4 * jax.random.normal(keys[3], (ORBS, BOX, BOX * BOX), jnp.float32)
    factor = jnp.ones((ORBS,), jnp.float32)
    total = noise
    for which in range(waves):
        chosen = modes[which]
        turns = chosen[:, 0, None, None] * cell_x[None, :, None] + chosen[:, 1, None, None] * cell_y[None, None, :] + chosen[:, 2, None, None] * cell_z[None, None, :]
        turns = turns % BOX
        angle = 2.0 * math.pi / BOX * turns.astype(jnp.float32) + phases[which][:, None, None]
        total = total + amplitude * factor[:, None, None] * jnp.cos(angle)
    return jnp.clip(total, -6.0, 6.0).astype(jnp.bfloat16)


def draw_pair_list(key, part):
    key = jax.random.fold_in(key, 11)
    keys = jax.random.split(key, 4)
    domains = DOM_X * DOM_Y
    index = jnp.arange(domains, dtype=jnp.int32)
    home_x = index // DOM_Y
    home_y = index % DOM_Y
    own_slot = jax.random.randint(keys[0], (domains, PAIR_DEV), 0, ORB_DEV)
    step_x = jax.random.randint(keys[1], (domains, PAIR_DEV), -1, 2)
    step_y = jax.random.randint(keys[2], (domains, PAIR_DEV), -1, 2)
    other_slot = jax.random.randint(keys[3], (domains, PAIR_DEV), 0, ORB_DEV)
    other_x = (home_x[:, None] + step_x) % DOM_X
    other_y = (home_y[:, None] + step_y) % DOM_Y
    first = index[:, None] * ORB_DEV + own_slot
    second = (other_x * DOM_Y + other_y) * ORB_DEV + other_slot
    return jnp.stack([first, second], axis=-1).reshape(PAIR_DEV * domains, 2).astype(jnp.int32)


def draw_pair_mask(key, part):
    key = jax.random.fold_in(key, 23)
    keys = jax.random.split(key, 3)
    domains = DOM_X * DOM_Y
    counts = jax.random.randint(keys[0], (domains,), 1, PAIR_DEV + 1)
    fullest = jax.random.randint(keys[1], (), 0, domains)
    counts = jnp.where(jnp.arange(domains) == fullest, PAIR_DEV, counts)
    orders = jax.vmap(lambda k: jax.random.permutation(k, PAIR_DEV))(jax.random.split(keys[2], domains))
    return (orders < counts[:, None]).astype(jnp.int32).reshape(PAIR_DEV * domains)


def plant(drawn, key, low, top_value):
    longest = drawn.shape.index(max(drawn.shape))
    spots = []
    for shift in (0, 1):
        where = [jax.random.randint(jax.random.fold_in(key, axis), (), 0, length) for axis, length in enumerate(drawn.shape)]
        where[longest] = (where[longest] + shift) % drawn.shape[longest]
        spots.append(tuple(where))
    return drawn.at[spots[0]].set(low).at[spots[1]].set(top_value)


def setup_inputs(seed: int = 0) -> dict:
    key_list = jax.random.split(jax.random.key(seed), 5)
    return {
        "orbitals": draw_orbitals(jax.random.fold_in(key_list[4], 71), 0),
        "offsets": plant(jax.random.randint(key_list[1], (ORBS, 3), 0, BOX // 2), jax.random.fold_in(key_list[1], 1), 0, (BOX // 2) - 1).astype(jnp.int32),
        "pair_list": draw_pair_list(jax.random.fold_in(key_list[4], 71), 0),
        "pair_mask": draw_pair_mask(jax.random.fold_in(key_list[4], 71), 0),
    }


def shift_box(field, sx, sy, sz):
    box = field.shape[0]
    flat = field.shape[1]
    padded = jnp.pad(field, ((box, box), (0, 0)))
    field = lax.dynamic_slice_in_dim(padded, (box + sx).astype(jnp.int32), box, 0)
    padded = jnp.pad(field, ((0, 0), (flat, flat)))
    field = lax.dynamic_slice_in_dim(padded, (flat + sy * box).astype(jnp.int32), flat, 1)
    padded = jnp.pad(field, ((0, 0), (box, box)))
    field = lax.dynamic_slice_in_dim(padded, (box + sz).astype(jnp.int32), flat, 1)
    column = jnp.arange(flat, dtype=jnp.int32) % box + sz
    keep = (column >= 0) & (column < box)
    return jnp.where(keep[None, :], field, jnp.zeros_like(field))


def kernel_table(box):
    freq = jnp.arange(box, dtype=jnp.int32)
    freq = freq - box * (freq >= box // 2).astype(jnp.int32)
    wave = (2.0 * math.pi / box) * freq.astype(jnp.float32)
    square = wave * wave
    total = square[:, None, None] + square[None, :, None] + square[None, None, :]
    return 1.0 / (total + (8.0 * math.pi / box) ** 2)


def reference(orbitals, offsets, pair_list, pair_mask):
    box = orbitals.shape[1]
    kernel = kernel_table(box)

    def visit(total, slot):
        first, second, valid = slot
        phi_first = orbitals[first].astype(jnp.float32)
        phi_second = orbitals[second].astype(jnp.float32)
        move = offsets[first] - offsets[second]
        partner = shift_box(phi_second, move[0], move[1], move[2])
        density = phi_first * partner * valid.astype(jnp.float32)
        spectrum = jnp.fft.fftn(density.reshape(box, box, box))
        potential = jnp.real(jnp.fft.ifftn(kernel * spectrum)).astype(jnp.float32).reshape(box, box * box)
        total = total.at[first].add(potential * partner)
        total = total.at[second].add(shift_box(potential * phi_first, -move[0], -move[1], -move[2]))
        return total, None

    start = jnp.zeros(orbitals.shape, jnp.float32)
    total, unused = lax.scan(visit, start, (pair_list[:, 0], pair_list[:, 1], pair_mask))
    return total
```

```python
import functools
import math

import jax
import jax.numpy as jnp
import ml_dtypes
import numpy as np
from jax import lax
from jax.experimental import pallas as pl
from jax.experimental.pallas import tpu as pltpu
from jax.sharding import PartitionSpec as P

GROUP = 8


def basis(box):
    half = box // 2
    index = np.arange(box)
    freq = np.where(index <= half, index, index - half)
    angle = 2.0 * np.pi / box * ((freq[:, None] * index[None, :]) % box)
    rows = np.where(index[:, None] <= half, np.cos(angle), np.sin(angle))
    scale = np.where((index == 0) | (index == half), 1.0, math.sqrt(2.0)) / math.sqrt(box)
    return rows * scale[:, None], freq


def split_np(value):
    high = value.astype(ml_dtypes.bfloat16)
    low = (value - high.astype(np.float64)).astype(ml_dtypes.bfloat16)
    return high, low


def left_table(matrix):
    high, low = split_np(matrix)
    return np.block([[high, high], [low, np.zeros_like(low)]])


def right_table(matrix):
    high, low = split_np(np.kron(np.eye(2), matrix))
    return np.block([[high, low], [high, np.zeros_like(low)]])


def tables(box):
    rows, freq = basis(box)
    wave = 2.0 * np.pi / box * freq
    square = (wave * wave).astype(np.float32)
    column = square[:, None] + np.zeros((1, 2 * box), np.float32)
    lane = np.concatenate([square, square])[None, :] + np.zeros((8, 1), np.float32)
    return (
        left_table(rows),
        left_table(rows.T),
        right_table(rows.T),
        right_table(rows),
        column,
        lane,
    )


def split(value):
    high = value.astype(jnp.bfloat16)
    low = (value - high.astype(jnp.float32)).astype(jnp.bfloat16)
    return high, low


def apply_left(table, tiles):
    box = tiles[0].shape[0]
    high, low = split(jnp.concatenate(tiles, axis=1))
    both = jnp.concatenate([high, low], axis=0)
    out = jnp.dot(table, both, preferred_element_type=jnp.float32)
    out = out[:box] + out[box:]
    return [out[:, 128 * i : 128 * (i + 1)] for i in range(len(tiles))]


def apply_right(table, tiles):
    box, lanes = tiles[0].shape
    high, low = split(jnp.concatenate(tiles, axis=0))
    both = jnp.concatenate([high, low], axis=1)
    out = jnp.dot(both, table, preferred_element_type=jnp.float32)
    out = out[:, :lanes] + out[:, lanes:]
    return [out[box * i : box * (i + 1)] for i in range(len(tiles))]


def placing(box, which, move_z):
    rows = lax.broadcasted_iota(jnp.int32, (4 * box, 8 * box), 0)
    cols = lax.broadcasted_iota(jnp.int32, (4 * box, 8 * box), 1)
    keep = (rows // box == cols // (2 * box)) & (rows % box == cols % box + move_z)
    if which is not None:
        keep = keep & ((cols // box) % 2 == which)
    return jnp.where(keep, 1.0, 0.0).astype(jnp.bfloat16)


def kernel(pairs, has_prev, box, *refs):
    units = 2 * pairs
    info, left_f, left_i, right_f, right_i, column, lane_sq, own = refs[:8]
    others = refs[8 : 8 + units]
    rest = refs[8 + units :]
    if has_prev:
        prev, rest = rest[0], rest[1:]
    out, staged, partner, work, total, phi, green = rest
    chunks = box // 4
    flat_rows = box * box

    lane = lax.broadcasted_iota(jnp.int32, (box, 2 * box), 1)
    low_half = lane < box

    staged[...] = jnp.zeros_like(staged)
    total[...] = jnp.zeros_like(total)
    place_own = placing(box, None, 0)

    def prepare(j, carry):
        part = own[:, pl.ds(pl.multiple_of(j * 4 * box, 4 * box), 4 * box)]
        res = jnp.dot(part, place_own, preferred_element_type=jnp.float32)
        for i in range(4):
            start = pl.multiple_of((4 * j + i) * box, box)
            phi[pl.ds(start, box), :] = res[:, 2 * box * i : 2 * box * (i + 1)]
            wx = column[pl.ds(4 * j + i, 1), :]
            sq = column[...] + lane_sq[0:1, :] + wx + (8.0 * math.pi / box) ** 2
            green[pl.ds(start, box), :] = 1.0 / sq
        return carry

    lax.fori_loop(0, chunks, prepare, 0)

    def one_pair(p, carry):
        unit_a, unit_b = 2 * p, 2 * p + 1
        count_a = info[unit_a, 3]
        count_b = info[unit_b, 3]

        @pl.when(count_a + count_b > 0)
        def _():
            place = jnp.concatenate(
                [placing(box, 0, info[unit_a, 2]), placing(box, 1, info[unit_b, 2])], axis=0
            )
            for q in range(pairs):

                @pl.when(p == q)
                def _():
                    def stage(j, inner):
                        here = pl.ds(pl.multiple_of(j * 4 * box, 4 * box), 4 * box)
                        part = jnp.concatenate(
                            [others[2 * q][:, here], others[2 * q + 1][:, here]], axis=1
                        )
                        res = jnp.dot(part, place, preferred_element_type=jnp.float32)
                        for i in range(4):
                            start = pl.multiple_of((4 * j + i) * 2 * box + box // 2, box // 2)
                            staged[pl.ds(start, box), :] = res[:, 2 * box * i : 2 * box * (i + 1)]
                        return inner

                    lax.fori_loop(0, chunks, stage, 0)

            def fetch(y, unit):
                source = y + info[unit, 1]
                inside = (source >= 0) & (source < box)
                row = jnp.clip(source, 0, box - 1) * 2 * box + box // 2 + info[unit, 0]
                return staged[pl.ds(row, box), :] * jnp.where(inside, 1.0, 0.0)

            def forward(g, inner):
                tiles = []
                for i in range(GROUP):
                    y = g * GROUP + i
                    start = pl.multiple_of(y * box, box)
                    moved = jnp.where(low_half, fetch(y, unit_a), fetch(y, unit_b))
                    partner[pl.ds(start, box), :] = moved
                    tiles.append(moved * phi[pl.ds(start, box), :])
                tiles = apply_right(right_f[...], apply_left(left_f[...], tiles))
                for i in range(GROUP):
                    start = pl.multiple_of((g * GROUP + i) * box, box)
                    work[pl.ds(start, box), :] = tiles[i]
                return inner

            lax.fori_loop(0, box // GROUP, forward, 0)

            def middle(g, inner):
                tiles = []
                for i in range(GROUP):
                    tiles.append(work[pl.ds(g * GROUP + i, box, stride=box), :])
                tiles = apply_left(left_f[...], tiles)
                for i in range(GROUP):
                    start = pl.multiple_of((g * GROUP + i) * box, box)
                    tiles[i] = tiles[i] * green[pl.ds(start, box), :]
                tiles = apply_left(left_i[...], tiles)
                for i in range(GROUP):
                    work[pl.ds(g * GROUP + i, box, stride=box), :] = tiles[i]
                return inner

            lax.fori_loop(0, box // GROUP, middle, 0)
            weight = jnp.where(low_half, count_a.astype(jnp.float32), count_b.astype(jnp.float32))

            def back(g, inner):
                tiles = []
                for i in range(GROUP):
                    start = pl.multiple_of((g * GROUP + i) * box, box)
                    tiles.append(work[pl.ds(start, box), :])
                tiles = apply_left(left_i[...], apply_right(right_i[...], tiles))
                for i in range(GROUP):
                    start = pl.multiple_of((g * GROUP + i) * box, box)
                    here = pl.ds(start, box)
                    total[here, :] = total[here, :] + tiles[i] * partner[here, :] * weight
                return inner

            lax.fori_loop(0, box // GROUP, back, 0)

        return carry

    lax.fori_loop(0, pairs, one_pair, 0)

    def finish(j, carry):
        even = total[pl.ds(pl.multiple_of(2 * j * box, box), box), :]
        odd = total[pl.ds(pl.multiple_of((2 * j + 1) * box, box), box), :]
        even = even + pltpu.roll(even, box, 1)
        odd = odd + pltpu.roll(odd, box, 1)
        res = jnp.where(low_half, even, odd)
        here = pl.ds(pl.multiple_of(j * 2 * box, 2 * box), 2 * box)
        if has_prev:
            res = res + prev[:, here]
        out[:, here] = res
        return carry

    lax.fori_loop(0, box // 2, finish, 0)


def pair_sum(info, consts, own, others, prev=None):
    box, flat = own.shape
    pairs = len(others) // 2
    vmem = pl.BlockSpec(memory_space=pltpu.VMEM)
    operands = [info, *consts, own, *others] + ([] if prev is None else [prev])
    specs = [pl.BlockSpec(memory_space=pltpu.SMEM)] + [vmem] * (len(operands) - 1)
    rows = box * box
    macs = pairs * 7 * 4096 * 65536
    return pl.pallas_call(
        functools.partial(kernel, pairs, prev is not None, box),
        out_shape=jax.ShapeDtypeStruct((box, flat), jnp.float32),
        in_specs=specs,
        out_specs=vmem,
        scratch_shapes=[pltpu.VMEM((2 * rows, 2 * box), jnp.float32)]
        + [pltpu.VMEM((rows, 2 * box), jnp.float32)] * 5,
        compiler_params=pltpu.CompilerParams(vmem_limit_bytes=48 * 1024 * 1024),
        cost_estimate=pl.CostEstimate(
            flops=2 * macs, bytes_accessed=pairs * 2 * rows * box * 2, transcendentals=0
        ),
    )(*operands)


def shifted(value, axis, steps):
    count = lax.axis_size(axis)
    pairs = [(source, (source + steps) % count) for source in range(count)]
    return lax.ppermute(value, axis, pairs)


def body(orbitals, offsets, pair_list, pair_mask):
    box = orbitals.shape[1]
    count_x = lax.axis_size("dx")
    count_y = lax.axis_size("dy")
    place_x = lax.axis_index("dx")
    place_y = lax.axis_index("dy")
    me = place_x * count_y + place_y
    own = orbitals[0]
    near = {(0, 0): own}
    for i in (-1, 1):
        near[i, 0] = shifted(own, "dx", -i)
    for i in (0, -1, 1):
        for j in (-1, 1):
            near[i, j] = shifted(near[i, 0], "dy", -j)

    cells = [(i, j) for i in (-1, 0, 1) for j in (-1, 0, 1)]
    mates = jnp.stack(
        [((place_x + i) % count_x) * count_y + (place_y + j) % count_y for i, j in cells]
    )
    second = pair_list[:, 1]
    mine = jnp.sum(
        jnp.where(second[None, :] == mates[:, None], pair_mask[None, :], 0), axis=1
    )
    every = lax.all_gather(mine, ("dx", "dy"), axis=0, tiled=False)
    every = every.reshape(count_x * count_y, len(cells))
    theirs = every[mates, len(cells) - 1 - jnp.arange(len(cells))]
    counts = mine + theirs
    move = offsets[me][None, :] - offsets[mates]
    info = jnp.concatenate([move, counts[:, None]], axis=1).astype(jnp.int32)
    nothing = jnp.zeros((1, 4), jnp.int32)
    info = jnp.concatenate([info, nothing], axis=0)

    consts = tuple(jnp.asarray(t) for t in tables(box))
    order = [(0, 0), None, (0, -1), (0, 1), (-1, 0), (1, 0), (-1, -1), (-1, 1), (1, -1), (1, 1)]
    pick = np.array([len(cells) if c is None else cells.index(c) for c in order])
    others = [own if c is None else near[c] for c in order]
    return pair_sum(info[pick], consts, own, others)[None]


def solution(mesh):
    placed = (P(("dx", "dy"), None, None), P(), P(("dx", "dy"), None), P(("dx", "dy")))
    return jax.shard_map(
        body, mesh=mesh, in_specs=placed, out_specs=P(("dx", "dy"), None, None), check_vma=False
    )
```

```python
import functools
import math

import jax
import jax.numpy as jnp
import ml_dtypes
import numpy as np
from jax import lax
from jax.experimental import pallas as pl
from jax.experimental.pallas import tpu as pltpu
from jax.sharding import PartitionSpec as P

GROUP = 8
CELLS = [(i, j) for i in (-1, 0, 1) for j in (-1, 0, 1)]
SLOTS = [cell for cell in CELLS if cell != (0, 0)]
ORDER = [(0, 0), (0, 0), (-1, 0), (1, 0), (0, -1), (0, 1), (-1, -1), (-1, 1), (1, -1), (1, 1)]
PAIRS = len(ORDER) // 2


def basis(box):
    half = box // 2
    index = np.arange(box)
    freq = np.where(index <= half, index, index - half)
    angle = 2.0 * np.pi / box * ((freq[:, None] * index[None, :]) % box)
    rows = np.where(index[:, None] <= half, np.cos(angle), np.sin(angle))
    scale = np.where((index == 0) | (index == half), 1.0, math.sqrt(2.0)) / math.sqrt(box)
    return rows * scale[:, None], freq


def split_np(value):
    high = value.astype(ml_dtypes.bfloat16)
    low = (value - high.astype(np.float64)).astype(ml_dtypes.bfloat16)
    return high, low


def left_table(matrix):
    high, low = split_np(matrix)
    return np.block([[high, high], [low, np.zeros_like(low)]])


def right_table(matrix):
    high, low = split_np(np.kron(np.eye(2), matrix))
    return np.block([[high, low], [high, np.zeros_like(low)]])


def tables(box):
    rows, freq = basis(box)
    wave = 2.0 * np.pi / box * freq
    square = (wave * wave).astype(np.float32)
    column = square[:, None] + np.zeros((1, 2 * box), np.float32)
    lane = np.concatenate([square, square])[None, :] + np.zeros((8, 1), np.float32)
    return (
        left_table(rows),
        left_table(rows.T),
        right_table(rows.T),
        right_table(rows),
        column,
        lane,
    )


def split(value):
    high = value.astype(jnp.bfloat16)
    low = (value - high.astype(jnp.float32)).astype(jnp.bfloat16)
    return high, low


def apply_left(table, tiles):
    box = tiles[0].shape[0]
    high, low = split(jnp.concatenate(tiles, axis=1))
    both = jnp.concatenate([high, low], axis=0)
    out = jnp.dot(table, both, preferred_element_type=jnp.float32)
    out = out[:box] + out[box:]
    return [out[:, 128 * i : 128 * (i + 1)] for i in range(len(tiles))]


def apply_right(table, tiles):
    box, lanes = tiles[0].shape
    high, low = split(jnp.concatenate(tiles, axis=0))
    both = jnp.concatenate([high, low], axis=1)
    out = jnp.dot(both, table, preferred_element_type=jnp.float32)
    out = out[:, :lanes] + out[:, lanes:]
    return [out[box * i : box * (i + 1)] for i in range(len(tiles))]


def placing(box, which, move_z):
    rows = lax.broadcasted_iota(jnp.int32, (4 * box, 8 * box), 0)
    cols = lax.broadcasted_iota(jnp.int32, (4 * box, 8 * box), 1)
    keep = (rows // box == cols // (2 * box)) & (rows % box == cols % box + move_z)
    if which is not None:
        keep = keep & ((cols // box) % 2 == which)
    return jnp.where(keep, 1.0, 0.0).astype(jnp.bfloat16)


def kernel(count_x, count_y, box, *refs):
    offsets, pair_list, pair_mask, left_f, left_i, right_f, right_i, column, lane_sq, own = refs[:10]
    out, staged, partner, work, total, phi, green = refs[10:17]
    tally, weights, moves, landed, landed_tally = refs[17:22]
    send_sem, recv_sem, tally_send, tally_recv = refs[22:]
    chunks = box // 4
    pitch = box + 8

    place_x = lax.axis_index("dx")
    place_y = lax.axis_index("dy")

    def domain(i, j):
        return lax.rem(place_x + i + count_x, count_x), lax.rem(place_y + j + count_y, count_y)

    def owner(i, j):
        x, y = domain(i, j)
        return x * count_y + y

    def target(i, j):
        x, y = domain(i, j)
        return {"dx": x} if j == 0 else {"dy": y}

    barrier = pltpu.get_barrier_semaphore()
    for step in ((1, 0), (-1, 0), (0, 1), (0, -1)):
        pl.semaphore_signal(
            barrier, inc=1, device_id=target(*step), device_id_type=pl.DeviceIdType.MESH
        )

    tally[...] = jnp.zeros_like(tally)
    for row, (i, j) in enumerate(CELLS):
        number = jnp.int32(0)
        for slot in range(pair_mask.shape[0]):
            same = pair_list[slot, 1] == owner(i, j)
            number = number + jnp.where(same, pair_mask[slot], 0)
        tally[row : row + 1, :] = jnp.full((1, 2 * box), 1.0, jnp.float32) * number.astype(
            jnp.float32
        )
    mine = owner(0, 0)
    for unit, cell in enumerate(ORDER):
        for axis in range(3):
            moves[unit, axis] = offsets[mine, axis] - offsets[owner(*cell), axis]

    pl.semaphore_wait(barrier, 4)

    def copies(source, i, j):
        slot = SLOTS.index((source[0] - i, source[1] - j))
        block, number = (own, tally)
        if source != (0, 0):
            block = landed.at[SLOTS.index(source)]
            number = landed_tally.at[SLOTS.index(source)]
        made = []
        for src, dst, send, recv in (
            (number, landed_tally, tally_send, tally_recv),
            (block, landed, send_sem, recv_sem),
        ):
            made.append(
                pltpu.make_async_remote_copy(
                    src_ref=src,
                    dst_ref=dst.at[slot],
                    send_sem=send.at[slot],
                    recv_sem=recv.at[slot],
                    device_id=target(i, j),
                    device_id_type=pl.DeviceIdType.MESH,
                )
            )
        return made

    first = [copies((0, 0), *step) for step in ((1, 0), (-1, 0), (0, 1), (0, -1))]
    relay = [copies((i, 0), 0, j) for i in (-1, 1) for j in (1, -1)]
    arrive = {(-1, 0): first[0], (1, 0): first[1], (0, -1): first[2], (0, 1): first[3]}
    arrive.update({(-1, -1): relay[0], (-1, 1): relay[1], (1, -1): relay[2], (1, 1): relay[3]})
    for pair in first:
        for copy in pair:
            copy.start()

    lane = lax.broadcasted_iota(jnp.int32, (box, 2 * box), 1)
    low_half = lane < box

    staged[...] = jnp.zeros_like(staged)
    total[...] = jnp.zeros_like(total)
    place_own = placing(box, None, 0)

    def prepare(j, carry):
        part = own[:, pl.ds(pl.multiple_of(j * 4 * box, 4 * box), 4 * box)]
        res = jnp.dot(part, place_own, preferred_element_type=jnp.float32)
        for i in range(4):
            start = pl.multiple_of((4 * j + i) * box, box)
            phi[pl.ds(start, box), :] = res[:, 2 * box * i : 2 * box * (i + 1)]
            wx = column[pl.ds(4 * j + i, 1), :]
            sq = column[...] + lane_sq[0:1, :] + wx + (8.0 * math.pi / box) ** 2
            green[pl.ds(start, box), :] = 1.0 / sq
        return carry

    lax.fori_loop(0, chunks, prepare, 0)

    def one_pair(p, carry):
        unit_a, unit_b = 2 * p, 2 * p + 1

        place = jnp.concatenate(
            [placing(box, 0, moves[unit_a, 2]), placing(box, 1, moves[unit_b, 2])], axis=0
        )
        for q in range(PAIRS):

            @pl.when(p == q)
            def _():
                cells = ORDER[2 * q : 2 * q + 2]
                blocks, rows = [], []
                for which, (i, j) in enumerate(cells):
                    row = CELLS.index((i, j))
                    if (i, j) == (0, 0):
                        blocks.append(own)
                        rows.append(tally[row : row + 1, :] * (2.0 if which == 0 else 0.0))
                        continue
                    slot = SLOTS.index((i, j))
                    for copy in arrive[i, j]:
                        copy.wait_recv()
                    blocks.append(landed.at[slot])
                    back_row = CELLS.index((-i, -j))
                    rows.append(
                        tally[row : row + 1, :] + landed_tally[slot, back_row : back_row + 1, :]
                    )
                if q == 1:
                    for pair in relay:
                        for copy in pair:
                            copy.start()
                weights[...] = jnp.where(low_half[0:8], rows[0], rows[1])

                def stage(j, inner):
                    here = pl.ds(pl.multiple_of(j * 4 * box, 4 * box), 4 * box)
                    part = jnp.concatenate([block[:, here] for block in blocks], axis=1)
                    res = jnp.dot(part, place, preferred_element_type=jnp.float32)
                    for i in range(4):
                        start = pl.multiple_of((4 * j + i) * 2 * box + box // 2, box // 2)
                        staged[pl.ds(start, box), :] = res[:, 2 * box * i : 2 * box * (i + 1)]
                    return inner

                lax.fori_loop(0, chunks, stage, 0)

        def fetch(y, unit):
            source = y + moves[unit, 1]
            inside = (source >= 0) & (source < box)
            row = jnp.clip(source, 0, box - 1) * 2 * box + box // 2 + moves[unit, 0]
            return staged[pl.ds(row, box), :] * jnp.where(inside, 1.0, 0.0)

        def forward(g, inner):
            tiles = []
            for i in range(GROUP):
                y = g * GROUP + i
                start = pl.multiple_of(y * box, box)
                moved = jnp.where(low_half, fetch(y, unit_a), fetch(y, unit_b))
                partner[pl.ds(start, box), :] = moved
                tiles.append(moved * phi[pl.ds(start, box), :])
            tiles = apply_right(right_f[...], apply_left(left_f[...], tiles))
            for i in range(GROUP):
                start = pl.multiple_of((g * GROUP + i) * pitch, 8)
                work[pl.ds(start, box), :] = tiles[i]
            return inner

        lax.fori_loop(0, box // GROUP, forward, 0)

        def middle(g, inner):
            tiles = []
            for i in range(GROUP):
                tiles.append(work[pl.ds(g * GROUP + i, box, stride=pitch), :])
            tiles = apply_left(left_f[...], tiles)
            for i in range(GROUP):
                start = pl.multiple_of((g * GROUP + i) * box, box)
                tiles[i] = tiles[i] * green[pl.ds(start, box), :]
            tiles = apply_left(left_i[...], tiles)
            for i in range(GROUP):
                work[pl.ds(g * GROUP + i, box, stride=pitch), :] = tiles[i]
            return inner

        lax.fori_loop(0, box // GROUP, middle, 0)

        def back(g, inner):
            tiles = []
            for i in range(GROUP):
                start = pl.multiple_of((g * GROUP + i) * pitch, 8)
                tiles.append(work[pl.ds(start, box), :])
            tiles = apply_left(left_i[...], apply_right(right_i[...], tiles))
            weight = weights[0:1, :]
            for i in range(GROUP):
                start = pl.multiple_of((g * GROUP + i) * box, box)
                here = pl.ds(start, box)
                total[here, :] = total[here, :] + tiles[i] * partner[here, :] * weight
            return inner

        lax.fori_loop(0, box // GROUP, back, 0)
        return carry

    lax.fori_loop(0, PAIRS, one_pair, 0)

    def finish(j, carry):
        even = total[pl.ds(pl.multiple_of(2 * j * box, box), box), :]
        odd = total[pl.ds(pl.multiple_of((2 * j + 1) * box, box), box), :]
        even = even + pltpu.roll(even, box, 1)
        odd = odd + pltpu.roll(odd, box, 1)
        here = pl.ds(pl.multiple_of(j * 2 * box, 2 * box), 2 * box)
        out[:, here] = jnp.where(low_half, even, odd)
        return carry

    lax.fori_loop(0, box // 2, finish, 0)
    for pair in first + relay:
        for copy in pair:
            copy.wait_send()


def body(orbitals, offsets, pair_list, pair_mask):
    box, flat = orbitals.shape[1:]
    consts = tuple(jnp.asarray(t) for t in tables(box))
    vmem = pl.BlockSpec(memory_space=pltpu.VMEM)
    smem = pl.BlockSpec(memory_space=pltpu.SMEM)
    rows = box * box
    macs = PAIRS * 7 * 4096 * 65536
    slots = len(SLOTS)
    out = pl.pallas_call(
        functools.partial(kernel, lax.axis_size("dx"), lax.axis_size("dy"), box),
        out_shape=jax.ShapeDtypeStruct((box, flat), jnp.float32),
        in_specs=[smem] * 3 + [vmem] * (len(consts) + 1),
        out_specs=vmem,
        scratch_shapes=[
            pltpu.VMEM((2 * rows, 2 * box), jnp.float32),
            pltpu.VMEM((rows, 2 * box), jnp.float32),
            pltpu.VMEM((box * (box + 8), 2 * box), jnp.float32),
            pltpu.VMEM((rows, 2 * box), jnp.float32),
            pltpu.VMEM((rows, 2 * box), jnp.float32),
            pltpu.VMEM((rows, 2 * box), jnp.float32),
            pltpu.VMEM((16, 2 * box), jnp.float32),
            pltpu.VMEM((8, 2 * box), jnp.float32),
            pltpu.SMEM((len(ORDER), 3), jnp.int32),
            pltpu.VMEM((slots, box, flat), jnp.bfloat16),
            pltpu.VMEM((slots, 16, 2 * box), jnp.float32),
        ]
        + [pltpu.SemaphoreType.DMA((slots,))] * 4,
        compiler_params=pltpu.CompilerParams(
            vmem_limit_bytes=48 * 1024 * 1024, collective_id=0, has_side_effects=True
        ),
        cost_estimate=pl.CostEstimate(
            flops=2 * macs, bytes_accessed=10 * rows * box * 2, transcendentals=0
        ),
    )(offsets, pair_list, pair_mask, *consts, orbitals[0])
    return out[None]


def solution(mesh):
    placed = (P(("dx", "dy"), None, None), P(), P(("dx", "dy"), None), P(("dx", "dy")))
    return jax.shard_map(
        body, mesh=mesh, in_specs=placed, out_specs=P(("dx", "dy"), None, None), check_vma=False
    )
```

```python
import functools
import math

import jax
import jax.numpy as jnp
import ml_dtypes
import numpy as np
from jax import lax
from jax.experimental import pallas as pl
from jax.experimental.pallas import tpu as pltpu
from jax.sharding import PartitionSpec as P

GROUP = 16
LEFT = 2
RIGHT = 8
CELLS = [(i, j) for i in (-1, 0, 1) for j in (-1, 0, 1)]
SLOTS = [cell for cell in CELLS if cell != (0, 0)]
ORDER = [(0, 0), (0, 0), (-1, 0), (1, 0), (0, -1), (0, 1), (-1, -1), (-1, 1), (1, -1), (1, 1)]
PAIRS = len(ORDER) // 2


def basis(box):
    half = box // 2
    index = np.arange(box)
    freq = np.where(index <= half, index, index - half)
    angle = 2.0 * np.pi / box * ((freq[:, None] * index[None, :]) % box)
    rows = np.where(index[:, None] <= half, np.cos(angle), np.sin(angle))
    scale = np.where((index == 0) | (index == half), 1.0, math.sqrt(2.0)) / math.sqrt(box)
    return rows * scale[:, None], freq


def split_np(value):
    high = value.astype(ml_dtypes.bfloat16)
    low = (value - high.astype(np.float64)).astype(ml_dtypes.bfloat16)
    return high, low


def left_table(matrix):
    high, low = split_np(matrix)
    return np.block([[high, high], [low, np.zeros_like(low)]])


def right_table(matrix):
    high, low = split_np(np.kron(np.eye(2), matrix))
    return np.block([[high, low], [high, np.zeros_like(low)]])


def tables(box):
    rows, freq = basis(box)
    lefts = np.concatenate([left_table(rows), left_table(rows.T)], axis=1)
    return np.concatenate([lefts, right_table(rows.T), right_table(rows)], axis=0)


def split(value):
    high = value.astype(jnp.bfloat16)
    low = (value - high.astype(jnp.float32)).astype(jnp.bfloat16)
    return high, low


def apply_left(table, tiles):
    box, lanes = tiles[0].shape
    made = []
    for first in range(0, len(tiles), LEFT):
        high, low = split(jnp.concatenate(tiles[first : first + LEFT], axis=1))
        both = jnp.concatenate([high, low], axis=0)
        out = jnp.dot(table, both, preferred_element_type=jnp.float32)
        out = out[:box] + out[box:]
        made += [out[:, lanes * i : lanes * (i + 1)] for i in range(LEFT)]
    return made


def apply_right(table, tiles):
    box, lanes = tiles[0].shape
    made = []
    for first in range(0, len(tiles), RIGHT):
        high, low = split(jnp.concatenate(tiles[first : first + RIGHT], axis=0))
        both = jnp.concatenate([high, low], axis=1)
        out = jnp.dot(both, table, preferred_element_type=jnp.float32)
        out = out[:, :lanes] + out[:, lanes:]
        made += [out[box * i : box * (i + 1)] for i in range(RIGHT)]
    return made


def placing(box, which, move_z):
    rows = lax.broadcasted_iota(jnp.int32, (4 * box, 8 * box), 0)
    cols = lax.broadcasted_iota(jnp.int32, (4 * box, 8 * box), 1)
    keep = (rows // box == cols // (2 * box)) & (rows % box == cols % box + move_z)
    if which is not None:
        keep = keep & ((cols // box) % 2 == which)
    return jnp.where(keep, 1.0, 0.0).astype(jnp.bfloat16)


def kernel(count_x, count_y, box, *refs):
    offsets_in, list_in, mask_in, table_in, own_in = refs[:5]
    out, staged, partner, work, total, phi, green = refs[5:12]
    tally, weights, moves, landed, landed_tally = refs[12:17]
    offsets, pair_list, pair_mask, table, own = refs[17:22]
    send_sem, recv_sem, tally_send, tally_recv, local_sem = refs[22:]
    chunks = box // 4
    pitch = box + 8

    place_x = lax.axis_index("dx")
    place_y = lax.axis_index("dy")

    def domain(i, j):
        return lax.rem(place_x + i + count_x, count_x), lax.rem(place_y + j + count_y, count_y)

    def owner(i, j):
        x, y = domain(i, j)
        return x * count_y + y

    def target(i, j):
        x, y = domain(i, j)
        return {"dx": x} if j == 0 else {"dy": y}

    barrier = pltpu.get_barrier_semaphore()
    for step in ((1, 0), (-1, 0), (0, 1), (0, -1)):
        pl.semaphore_signal(
            barrier, inc=1, device_id=target(*step), device_id_type=pl.DeviceIdType.MESH
        )

    local = [
        pltpu.make_async_copy(src, dst, local_sem.at[k])
        for k, (src, dst) in enumerate(
            (
                (offsets_in, offsets),
                (list_in, pair_list),
                (mask_in, pair_mask),
                (own_in, own),
                (table_in, table),
            )
        )
    ]
    for copy in local:
        copy.start()
    tally[...] = jnp.zeros_like(tally)
    for copy in local[:3]:
        copy.wait()
    for row, (i, j) in enumerate(CELLS):
        number = jnp.int32(0)
        for slot in range(pair_mask.shape[0]):
            same = pair_list[1, slot] == owner(i, j)
            number = number + jnp.where(same, pair_mask[slot], 0)
        tally[row : row + 1, :] = jnp.full((1, 2 * box), 1.0, jnp.float32) * number.astype(
            jnp.float32
        )
    mine = owner(0, 0)
    for unit, cell in enumerate(ORDER):
        for axis in range(3):
            moves[unit, axis] = offsets[axis, mine] - offsets[axis, owner(*cell)]

    pl.semaphore_wait(barrier, 4)

    def copies(source, i, j):
        slot = SLOTS.index((source[0] - i, source[1] - j))
        block, number = (own_in, tally)
        if source != (0, 0):
            block = landed.at[SLOTS.index(source)]
            number = landed_tally.at[SLOTS.index(source)]
        made = []
        for src, dst, send, recv in (
            (block, landed, send_sem, recv_sem),
            (number, landed_tally, tally_send, tally_recv),
        ):
            made.append(
                pltpu.make_async_remote_copy(
                    src_ref=src,
                    dst_ref=dst.at[slot],
                    send_sem=send.at[slot],
                    recv_sem=recv.at[slot],
                    device_id=target(i, j),
                    device_id_type=pl.DeviceIdType.MESH,
                )
            )
        return made

    first = [copies((0, 0), *step) for step in ((1, 0), (-1, 0), (0, 1), (0, -1))]
    relay = [copies((i, 0), 0, j) for i in (-1, 1) for j in (1, -1)]
    arrive = {(-1, 0): first[0], (1, 0): first[1], (0, -1): first[2], (0, 1): first[3]}
    arrive.update({(-1, -1): relay[0], (-1, 1): relay[1], (1, -1): relay[2], (1, 1): relay[3]})
    for pair in first:
        for copy in pair:
            copy.start()

    lane = lax.broadcasted_iota(jnp.int32, (box, 2 * box), 1)
    low_half = lane < box

    staged[...] = jnp.zeros_like(staged)
    total[...] = jnp.zeros_like(total)
    place_own = placing(box, None, 0)

    def square(index):
        freq = jnp.where(index <= box // 2, index, index - box // 2).astype(jnp.float32)
        return (2.0 * math.pi / box * freq) * (2.0 * math.pi / box * freq)

    plane = square(lax.broadcasted_iota(jnp.int32, (box, 2 * box), 0))
    plane = plane + square(jnp.where(low_half, lane, lane - box)) + (8.0 * math.pi / box) ** 2
    local[3].wait()

    def prepare(j, carry):
        part = own[:, pl.ds(pl.multiple_of(j * 4 * box, 4 * box), 4 * box)]
        res = jnp.dot(part, place_own, preferred_element_type=jnp.float32)
        for i in range(4):
            start = pl.multiple_of((4 * j + i) * box, box)
            phi[pl.ds(start, box), :] = res[:, 2 * box * i : 2 * box * (i + 1)]
            green[pl.ds(start, box), :] = 1.0 / (plane + square(4 * j + i))
        return carry

    lax.fori_loop(0, chunks, prepare, 0)
    local[4].wait()
    left_f = table.at[0 : 2 * box, 0 : 2 * box]
    left_i = table.at[0 : 2 * box, 2 * box : 4 * box]
    right_f = table.at[2 * box : 6 * box, :]
    right_i = table.at[6 * box : 10 * box, :]

    def one_pair(p, carry):
        unit_a, unit_b = 2 * p, 2 * p + 1

        place = jnp.concatenate(
            [placing(box, 0, moves[unit_a, 2]), placing(box, 1, moves[unit_b, 2])], axis=0
        )
        for q in range(PAIRS):

            @pl.when(p == q)
            def _():
                cells = ORDER[2 * q : 2 * q + 2]
                blocks, rows = [], []
                for which, (i, j) in enumerate(cells):
                    row = CELLS.index((i, j))
                    if (i, j) == (0, 0):
                        blocks.append(own)
                        rows.append(tally[row : row + 1, :] * (2.0 if which == 0 else 0.0))
                        continue
                    slot = SLOTS.index((i, j))
                    for copy in arrive[i, j]:
                        copy.wait_recv()
                    blocks.append(landed.at[slot])
                    back_row = CELLS.index((-i, -j))
                    rows.append(
                        tally[row : row + 1, :] + landed_tally[slot, back_row : back_row + 1, :]
                    )
                if q == 1:
                    for pair in relay:
                        for copy in pair:
                            copy.start()
                weights[...] = jnp.where(low_half[0:8], rows[0], rows[1])

                def stage(j, inner):
                    here = pl.ds(pl.multiple_of(j * 4 * box, 4 * box), 4 * box)
                    part = jnp.concatenate([block[:, here] for block in blocks], axis=1)
                    res = jnp.dot(part, place, preferred_element_type=jnp.float32)
                    for i in range(4):
                        start = pl.multiple_of((4 * j + i) * 2 * box + box // 2, box // 2)
                        staged[pl.ds(start, box), :] = res[:, 2 * box * i : 2 * box * (i + 1)]
                    return inner

                lax.fori_loop(0, chunks, stage, 0)

        def fetch(y, unit):
            source = y + moves[unit, 1]
            inside = (source >= 0) & (source < box)
            row = jnp.clip(source, 0, box - 1) * 2 * box + box // 2 + moves[unit, 0]
            return staged[pl.ds(row, box), :] * jnp.where(inside, 1.0, 0.0)

        def forward(g, inner):
            tiles = []
            for i in range(GROUP):
                y = g * GROUP + i
                start = pl.multiple_of(y * box, box)
                moved = jnp.where(low_half, fetch(y, unit_a), fetch(y, unit_b))
                partner[pl.ds(start, box), :] = moved
                tiles.append(moved * phi[pl.ds(start, box), :])
            tiles = apply_right(right_f[...], apply_left(left_f[...], tiles))
            for i in range(GROUP):
                start = pl.multiple_of((g * GROUP + i) * pitch, 8)
                work[pl.ds(start, box), :] = tiles[i]
            return inner

        lax.fori_loop(0, box // GROUP, forward, 0)

        def middle(g, inner):
            tiles = []
            for i in range(GROUP):
                tiles.append(work[pl.ds(g * GROUP + i, box, stride=pitch), :])
            tiles = apply_left(left_f[...], tiles)
            for i in range(GROUP):
                start = pl.multiple_of((g * GROUP + i) * box, box)
                tiles[i] = tiles[i] * green[pl.ds(start, box), :]
            tiles = apply_left(left_i[...], tiles)
            for i in range(GROUP):
                work[pl.ds(g * GROUP + i, box, stride=pitch), :] = tiles[i]
            return inner

        lax.fori_loop(0, box // GROUP, middle, 0)

        def back(g, inner):
            tiles = []
            for i in range(GROUP):
                start = pl.multiple_of((g * GROUP + i) * pitch, 8)
                tiles.append(work[pl.ds(start, box), :])
            tiles = apply_left(left_i[...], apply_right(right_i[...], tiles))
            weight = weights[0:1, :]
            for i in range(GROUP):
                start = pl.multiple_of((g * GROUP + i) * box, box)
                here = pl.ds(start, box)
                total[here, :] = total[here, :] + tiles[i] * partner[here, :] * weight
            return inner

        lax.fori_loop(0, box // GROUP, back, 0)
        return carry

    lax.fori_loop(0, PAIRS, one_pair, 0)

    def finish(j, carry):
        even = total[pl.ds(pl.multiple_of(2 * j * box, box), box), :]
        odd = total[pl.ds(pl.multiple_of((2 * j + 1) * box, box), box), :]
        even = even + pltpu.roll(even, box, 1)
        odd = odd + pltpu.roll(odd, box, 1)
        here = pl.ds(pl.multiple_of(j * 2 * box, 2 * box), 2 * box)
        out[:, here] = jnp.where(low_half, even, odd)
        return carry

    lax.fori_loop(0, box // 2, finish, 0)
    for pair in first + relay:
        for copy in pair:
            copy.wait_send()


def body(orbitals, offsets, pair_list, pair_mask):
    box, flat = orbitals.shape[1:]
    table = jnp.asarray(tables(box))
    vmem = pl.BlockSpec(memory_space=pltpu.VMEM)
    stay = pl.BlockSpec(memory_space=pl.ANY)
    rows = box * box
    macs = PAIRS * 7 * 4096 * 65536
    slots = len(SLOTS)
    out = pl.pallas_call(
        functools.partial(kernel, lax.axis_size("dx"), lax.axis_size("dy"), box),
        out_shape=jax.ShapeDtypeStruct((box, flat), jnp.float32),
        in_specs=[stay] * 5,
        out_specs=vmem,
        scratch_shapes=[
            pltpu.VMEM((2 * rows, 2 * box), jnp.float32),
            pltpu.VMEM((rows, 2 * box), jnp.float32),
            pltpu.VMEM((box * (box + 8), 2 * box), jnp.float32),
            pltpu.VMEM((rows, 2 * box), jnp.float32),
            pltpu.VMEM((rows, 2 * box), jnp.float32),
            pltpu.VMEM((rows, 2 * box), jnp.float32),
            pltpu.VMEM((16, 2 * box), jnp.float32),
            pltpu.VMEM((8, 2 * box), jnp.float32),
            pltpu.SMEM((len(ORDER), 3), jnp.int32),
            pltpu.VMEM((slots, box, flat), jnp.bfloat16),
            pltpu.VMEM((slots, 16, 2 * box), jnp.float32),
            pltpu.SMEM(offsets.shape[::-1], jnp.int32),
            pltpu.SMEM(pair_list.shape[::-1], jnp.int32),
            pltpu.SMEM(pair_mask.shape, jnp.int32),
            pltpu.VMEM(table.shape, jnp.bfloat16),
            pltpu.VMEM((box, flat), jnp.bfloat16),
        ]
        + [pltpu.SemaphoreType.DMA((slots,))] * 4
        + [pltpu.SemaphoreType.DMA((5,))],
        compiler_params=pltpu.CompilerParams(
            vmem_limit_bytes=60 * 1024 * 1024, collective_id=0, has_side_effects=True
        ),
        cost_estimate=pl.CostEstimate(
            flops=2 * macs, bytes_accessed=10 * rows * box * 2, transcendentals=0
        ),
    )(offsets.T, pair_list.T, pair_mask, table, orbitals[0])
    return out[None]


def solution(mesh):
    placed = (P(("dx", "dy"), None, None), P(), P(("dx", "dy"), None), P(("dx", "dy")))
    return jax.shard_map(
        body, mesh=mesh, in_specs=placed, out_specs=P(("dx", "dy"), None, None), check_vma=False
    )
```

```python
import functools
import math

import jax
import jax.numpy as jnp
import ml_dtypes
import numpy as np
from jax import lax
from jax.experimental import pallas as pl
from jax.experimental.pallas import tpu as pltpu
from jax.sharding import PartitionSpec as P

GROUP = 16
LEFT = 2
RIGHT = 8
CHUNKS = 8
CELLS = [(i, j) for i in (-1, 0, 1) for j in (-1, 0, 1)]
SLOTS = [cell for cell in CELLS if cell != (0, 0)]
ORDER = [(0, 0), (0, 0), (0, -1), (0, 1), (-1, 0), (1, 0), (-1, -1), (-1, 1), (1, -1), (1, 1)]
PAIRS = len(ORDER) // 2


def basis(box):
    half = box // 2
    index = np.arange(box)
    freq = np.where(index <= half, index, index - half)
    angle = 2.0 * np.pi / box * ((freq[:, None] * index[None, :]) % box)
    rows = np.where(index[:, None] <= half, np.cos(angle), np.sin(angle))
    scale = np.where((index == 0) | (index == half), 1.0, math.sqrt(2.0)) / math.sqrt(box)
    return rows * scale[:, None], freq


def split_np(value):
    high = value.astype(ml_dtypes.bfloat16)
    low = (value - high.astype(np.float64)).astype(ml_dtypes.bfloat16)
    return high, low


def left_table(matrix):
    high, low = split_np(matrix)
    return np.block([[high, high], [low, np.zeros_like(low)]])


def right_table(matrix):
    high, low = split_np(np.kron(np.eye(2), matrix))
    return np.block([[high, low], [high, np.zeros_like(low)]])


def tables(box):
    rows, freq = basis(box)
    lefts = np.concatenate([left_table(rows), left_table(rows.T)], axis=1)
    return np.concatenate([lefts, right_table(rows.T), right_table(rows)], axis=0)


def split(value):
    high = value.astype(jnp.bfloat16)
    low = (value - high.astype(jnp.float32)).astype(jnp.bfloat16)
    return high, low


def apply_left(table, tiles):
    box, lanes = tiles[0].shape
    made = []
    for first in range(0, len(tiles), LEFT):
        high, low = split(jnp.concatenate(tiles[first : first + LEFT], axis=1))
        both = jnp.concatenate([high, low], axis=0)
        out = jnp.dot(table, both, preferred_element_type=jnp.float32)
        out = out[:box] + out[box:]
        made += [out[:, lanes * i : lanes * (i + 1)] for i in range(LEFT)]
    return made


def apply_right(table, tiles):
    box, lanes = tiles[0].shape
    made = []
    for first in range(0, len(tiles), RIGHT):
        high, low = split(jnp.concatenate(tiles[first : first + RIGHT], axis=0))
        both = jnp.concatenate([high, low], axis=1)
        out = jnp.dot(both, table, preferred_element_type=jnp.float32)
        out = out[:, :lanes] + out[:, lanes:]
        made += [out[box * i : box * (i + 1)] for i in range(RIGHT)]
    return made


def placing(box, which, move_z):
    rows = lax.broadcasted_iota(jnp.int32, (4 * box, 8 * box), 0)
    cols = lax.broadcasted_iota(jnp.int32, (4 * box, 8 * box), 1)
    keep = (rows // box == cols // (2 * box)) & (rows % box == cols % box + move_z)
    if which is not None:
        keep = keep & ((cols // box) % 2 == which)
    return jnp.where(keep, 1.0, 0.0).astype(jnp.bfloat16)


def kernel(count_x, count_y, box, *refs):
    offsets_in, list_in, mask_in, table_in, own_in = refs[:5]
    out, staged, partner, work, total, phi, green = refs[5:12]
    tally, weights, moves, landed, landed_tally = refs[12:17]
    offsets, pair_list, pair_mask, table, own = refs[17:22]
    send_sem, recv_sem, tally_send, tally_recv, local_sem = refs[22:]
    chunks = box // 4
    pitch = box + 8

    place_x = lax.axis_index("dx")
    place_y = lax.axis_index("dy")

    def domain(i, j):
        return lax.rem(place_x + i + count_x, count_x), lax.rem(place_y + j + count_y, count_y)

    def owner(i, j):
        x, y = domain(i, j)
        return x * count_y + y

    def target(i, j):
        x, y = domain(i, j)
        return {"dx": x} if j == 0 else {"dy": y}

    barrier = pltpu.get_barrier_semaphore()
    for step in ((1, 0), (-1, 0), (0, 1), (0, -1)):
        pl.semaphore_signal(
            barrier, inc=1, device_id=target(*step), device_id_type=pl.DeviceIdType.MESH
        )

    local = [
        pltpu.make_async_copy(src, dst, local_sem.at[k])
        for k, (src, dst) in enumerate(
            (
                (offsets_in, offsets),
                (list_in, pair_list),
                (mask_in, pair_mask),
                (own_in, own),
                (table_in, table),
            )
        )
    ]
    for copy in local:
        copy.start()
    tally[...] = jnp.zeros_like(tally)
    for copy in local[:3]:
        copy.wait()
    for row, (i, j) in enumerate(CELLS):
        number = jnp.int32(0)
        for slot in range(pair_mask.shape[0]):
            same = pair_list[1, slot] == owner(i, j)
            number = number + jnp.where(same, pair_mask[slot], 0)
        tally[row : row + 1, :] = jnp.full((1, 2 * box), 1.0, jnp.float32) * number.astype(
            jnp.float32
        )
    mine = owner(0, 0)
    for unit, cell in enumerate(ORDER):
        for axis in range(3):
            moves[unit, axis] = offsets[axis, mine] - offsets[axis, owner(*cell)]

    pl.semaphore_wait(barrier, 4)

    def copies(source, i, j):
        slot = SLOTS.index((source[0] - i, source[1] - j))
        block, number = (own_in, tally)
        if source != (0, 0):
            block = landed.at[SLOTS.index(source)]
            number = landed_tally.at[SLOTS.index(source)]
        made = []
        for src, dst, send, recv in (
            (block, landed, send_sem, recv_sem),
            (number, landed_tally, tally_send, tally_recv),
        ):
            made.append(
                pltpu.make_async_remote_copy(
                    src_ref=src,
                    dst_ref=dst.at[slot],
                    send_sem=send.at[slot],
                    recv_sem=recv.at[slot],
                    device_id=target(i, j),
                    device_id_type=pl.DeviceIdType.MESH,
                )
            )
        return made

    first = [copies((0, 0), *step) for step in ((1, 0), (-1, 0), (0, 1), (0, -1))]
    relay = [copies((i, 0), 0, j) for i in (-1, 1) for j in (1, -1)]
    arrive = {(-1, 0): first[0], (1, 0): first[1], (0, -1): first[2], (0, 1): first[3]}
    arrive.update({(-1, -1): relay[0], (-1, 1): relay[1], (1, -1): relay[2], (1, 1): relay[3]})
    for pair in first:
        for copy in pair:
            copy.start()

    lane = lax.broadcasted_iota(jnp.int32, (box, 2 * box), 1)
    low_half = lane < box

    staged[...] = jnp.zeros_like(staged)
    total[...] = jnp.zeros_like(total)
    place_own = placing(box, None, 0)

    def square(index):
        freq = jnp.where(index <= box // 2, index, index - box // 2).astype(jnp.float32)
        return (2.0 * math.pi / box * freq) * (2.0 * math.pi / box * freq)

    plane = square(lax.broadcasted_iota(jnp.int32, (box, 2 * box), 0))
    plane = plane + square(jnp.where(low_half, lane, lane - box)) + (8.0 * math.pi / box) ** 2
    local[3].wait()

    def placed(j, blocks, table, write):
        parts = []
        for c in range(CHUNKS):
            here = pl.ds(pl.multiple_of((j * CHUNKS + c) * 4 * box, 4 * box), 4 * box)
            parts.append(jnp.concatenate([block[:, here] for block in blocks], axis=1))
        res = jnp.dot(jnp.concatenate(parts, axis=0), table, preferred_element_type=jnp.float32)
        for c in range(CHUNKS):
            for i in range(4):
                y = (j * CHUNKS + c) * 4 + i
                write(y, res[box * c : box * (c + 1), 2 * box * i : 2 * box * (i + 1)])

    def prepare(j, carry):
        def write(y, tile):
            start = pl.multiple_of(y * box, box)
            phi[pl.ds(start, box), :] = tile
            green[pl.ds(start, box), :] = 1.0 / (plane + square(y))

        placed(j, [own], place_own, write)
        return carry

    lax.fori_loop(0, chunks // CHUNKS, prepare, 0)
    local[4].wait()
    left_f = table.at[0 : 2 * box, 0 : 2 * box]
    left_i = table.at[0 : 2 * box, 2 * box : 4 * box]
    right_f = table.at[2 * box : 6 * box, :]
    right_i = table.at[6 * box : 10 * box, :]

    def one_pair(p, carry):
        unit_a, unit_b = 2 * p, 2 * p + 1

        place = jnp.concatenate(
            [placing(box, 0, moves[unit_a, 2]), placing(box, 1, moves[unit_b, 2])], axis=0
        )
        for q in range(PAIRS):

            @pl.when(p == q)
            def _():
                cells = ORDER[2 * q : 2 * q + 2]
                blocks, rows = [], []
                for which, (i, j) in enumerate(cells):
                    row = CELLS.index((i, j))
                    if (i, j) == (0, 0):
                        blocks.append(own)
                        rows.append(tally[row : row + 1, :] * (2.0 if which == 0 else 0.0))
                        continue
                    slot = SLOTS.index((i, j))
                    if j != 0:
                        for copy in arrive[i, j]:
                            copy.wait_recv()
                    blocks.append(landed.at[slot])
                    back_row = CELLS.index((-i, -j))
                    rows.append(
                        tally[row : row + 1, :] + landed_tally[slot, back_row : back_row + 1, :]
                    )
                weights[...] = jnp.where(low_half[0:8], rows[0], rows[1])

                def stage(j, inner):
                    def write(y, tile):
                        start = pl.multiple_of(y * 2 * box + box // 2, box // 2)
                        staged[pl.ds(start, box), :] = tile

                    placed(j, blocks, place, write)
                    return inner

                lax.fori_loop(0, chunks // CHUNKS, stage, 0)

        def fetch(y, unit):
            source = y + moves[unit, 1]
            inside = (source >= 0) & (source < box)
            row = jnp.clip(source, 0, box - 1) * 2 * box + box // 2 + moves[unit, 0]
            return staged[pl.ds(row, box), :] * jnp.where(inside, 1.0, 0.0)

        def forward(g, inner):
            tiles = []
            for i in range(GROUP):
                y = g * GROUP + i
                start = pl.multiple_of(y * box, box)
                moved = jnp.where(low_half, fetch(y, unit_a), fetch(y, unit_b))
                partner[pl.ds(start, box), :] = moved
                tiles.append(moved * phi[pl.ds(start, box), :])
            tiles = apply_right(right_f[...], apply_left(left_f[...], tiles))
            for i in range(GROUP):
                start = pl.multiple_of((g * GROUP + i) * pitch, 8)
                work[pl.ds(start, box), :] = tiles[i]
            return inner

        lax.fori_loop(0, box // GROUP, forward, 0)

        @pl.when(p == 1)
        def _():
            for k, i in enumerate((-1, 1)):
                for copy in arrive[i, 0]:
                    copy.wait_recv()
                for pair in relay[2 * k : 2 * k + 2]:
                    for copy in pair:
                        copy.start()

        def middle(g, inner):
            tiles = []
            for i in range(GROUP):
                tiles.append(work[pl.ds(g * GROUP + i, box, stride=pitch), :])
            tiles = apply_left(left_f[...], tiles)
            for i in range(GROUP):
                start = pl.multiple_of((g * GROUP + i) * box, box)
                tiles[i] = tiles[i] * green[pl.ds(start, box), :]
            tiles = apply_left(left_i[...], tiles)
            for i in range(GROUP):
                work[pl.ds(g * GROUP + i, box, stride=pitch), :] = tiles[i]
            return inner

        lax.fori_loop(0, box // GROUP, middle, 0)

        def back(g, inner):
            tiles = []
            for i in range(GROUP):
                start = pl.multiple_of((g * GROUP + i) * pitch, 8)
                tiles.append(work[pl.ds(start, box), :])
            tiles = apply_left(left_i[...], apply_right(right_i[...], tiles))
            weight = weights[0:1, :]
            for i in range(GROUP):
                start = pl.multiple_of((g * GROUP + i) * box, box)
                here = pl.ds(start, box)
                total[here, :] = total[here, :] + tiles[i] * partner[here, :] * weight
            return inner

        lax.fori_loop(0, box // GROUP, back, 0)
        return carry

    lax.fori_loop(0, PAIRS, one_pair, 0)

    def finish(j, carry):
        even = total[pl.ds(pl.multiple_of(2 * j * box, box), box), :]
        odd = total[pl.ds(pl.multiple_of((2 * j + 1) * box, box), box), :]
        even = even + pltpu.roll(even, box, 1)
        odd = odd + pltpu.roll(odd, box, 1)
        here = pl.ds(pl.multiple_of(j * 2 * box, 2 * box), 2 * box)
        out[:, here] = jnp.where(low_half, even, odd)
        return carry

    lax.fori_loop(0, box // 2, finish, 0)
    for pair in first + relay:
        for copy in pair:
            copy.wait_send()


def body(orbitals, offsets, pair_list, pair_mask):
    box, flat = orbitals.shape[1:]
    table = jnp.asarray(tables(box))
    vmem = pl.BlockSpec(memory_space=pltpu.VMEM)
    stay = pl.BlockSpec(memory_space=pl.ANY)
    rows = box * box
    macs = PAIRS * 7 * 4096 * 65536
    slots = len(SLOTS)
    out = pl.pallas_call(
        functools.partial(kernel, lax.axis_size("dx"), lax.axis_size("dy"), box),
        out_shape=jax.ShapeDtypeStruct((box, flat), jnp.float32),
        in_specs=[stay] * 5,
        out_specs=vmem,
        scratch_shapes=[
            pltpu.VMEM((2 * rows, 2 * box), jnp.float32),
            pltpu.VMEM((rows, 2 * box), jnp.float32),
            pltpu.VMEM((box * (box + 8), 2 * box), jnp.float32),
            pltpu.VMEM((rows, 2 * box), jnp.float32),
            pltpu.VMEM((rows, 2 * box), jnp.float32),
            pltpu.VMEM((rows, 2 * box), jnp.float32),
            pltpu.VMEM((16, 2 * box), jnp.float32),
            pltpu.VMEM((8, 2 * box), jnp.float32),
            pltpu.SMEM((len(ORDER), 3), jnp.int32),
            pltpu.VMEM((slots, box, flat), jnp.bfloat16),
            pltpu.VMEM((slots, 16, 2 * box), jnp.float32),
            pltpu.SMEM(offsets.shape[::-1], jnp.int32),
            pltpu.SMEM(pair_list.shape[::-1], jnp.int32),
            pltpu.SMEM(pair_mask.shape, jnp.int32),
            pltpu.VMEM(table.shape, jnp.bfloat16),
            pltpu.VMEM((box, flat), jnp.bfloat16),
        ]
        + [pltpu.SemaphoreType.DMA((slots,))] * 4
        + [pltpu.SemaphoreType.DMA((5,))],
        compiler_params=pltpu.CompilerParams(
            vmem_limit_bytes=60 * 1024 * 1024, collective_id=0, has_side_effects=True
        ),
        cost_estimate=pl.CostEstimate(
            flops=2 * macs, bytes_accessed=10 * rows * box * 2, transcendentals=0
        ),
    )(offsets.T, pair_list.T, pair_mask, table, orbitals[0])
    return out[None]


def solution(mesh):
    placed = (P(("dx", "dy"), None, None), P(), P(("dx", "dy"), None), P(("dx", "dy")))
    return jax.shard_map(
        body, mesh=mesh, in_specs=placed, out_specs=P(("dx", "dy"), None, None), check_vma=False
    )
```

```python
import functools
import math

import jax
import jax.numpy as jnp
import ml_dtypes
import numpy as np
from jax import lax
from jax.experimental import pallas as pl
from jax.experimental.pallas import tpu as pltpu
from jax.sharding import PartitionSpec as P

GROUP = 16
LEFT = 2
RIGHT = 8
CHUNKS = 8
CELLS = [(i, j) for i in (-1, 0, 1) for j in (-1, 0, 1)]
PAIRS = 5


def basis(box):
    half = box // 2
    index = np.arange(box)
    freq = np.where(index <= half, index, index - half)
    angle = 2.0 * np.pi / box * ((freq[:, None] * index[None, :]) % box)
    rows = np.where(index[:, None] <= half, np.cos(angle), np.sin(angle))
    scale = np.where((index == 0) | (index == half), 1.0, math.sqrt(2.0)) / math.sqrt(box)
    return rows * scale[:, None], freq


def split_np(value):
    high = value.astype(ml_dtypes.bfloat16)
    low = (value - high.astype(np.float64)).astype(ml_dtypes.bfloat16)
    return high, low


def left_table(matrix):
    high, low = split_np(matrix)
    return np.block([[high, high], [low, np.zeros_like(low)]])


def right_table(matrix):
    high, low = split_np(np.kron(np.eye(2), matrix))
    return np.block([[high, low], [high, np.zeros_like(low)]])


def tables(box):
    rows, freq = basis(box)
    lefts = np.concatenate([left_table(rows), left_table(rows.T)], axis=1)
    return np.concatenate([lefts, right_table(rows.T), right_table(rows)], axis=0)


def split(value):
    high = value.astype(jnp.bfloat16)
    low = (value - high.astype(jnp.float32)).astype(jnp.bfloat16)
    return high, low


def apply_left(table, tiles):
    box, lanes = tiles[0].shape
    made = []
    for first in range(0, len(tiles), LEFT):
        high, low = split(jnp.concatenate(tiles[first : first + LEFT], axis=1))
        both = jnp.concatenate([high, low], axis=0)
        out = jnp.dot(table, both, preferred_element_type=jnp.float32)
        out = out[:box] + out[box:]
        made += [out[:, lanes * i : lanes * (i + 1)] for i in range(LEFT)]
    return made


def apply_right(table, tiles):
    box, lanes = tiles[0].shape
    made = []
    for first in range(0, len(tiles), RIGHT):
        high, low = split(jnp.concatenate(tiles[first : first + RIGHT], axis=0))
        both = jnp.concatenate([high, low], axis=1)
        out = jnp.dot(both, table, preferred_element_type=jnp.float32)
        out = out[:, :lanes] + out[:, lanes:]
        made += [out[box * i : box * (i + 1)] for i in range(RIGHT)]
    return made


def placing(box, which, move_z):
    rows = lax.broadcasted_iota(jnp.int32, (4 * box, 8 * box), 0)
    cols = lax.broadcasted_iota(jnp.int32, (4 * box, 8 * box), 1)
    keep = (rows // box == cols // (2 * box)) & (rows % box == cols % box + move_z)
    if which is not None:
        keep = keep & ((cols // box) % 2 == which)
    return jnp.where(keep, 1.0, 0.0).astype(jnp.bfloat16)


def kernel(count_x, count_y, box, *refs):
    offsets_in, list_in, mask_in, table_in, own_in = refs[:5]
    out, staged, partner, work, total, phi, green = refs[5:12]
    tally, weights, moves, landed, landed_tally = refs[12:17]
    offsets, pair_list, pair_mask, table, own = refs[17:22]
    send_sem, recv_sem, tally_send, tally_recv, local_sem = refs[22:]
    chunks = box // 4
    pitch = box + 8

    place_x = lax.axis_index("dx")
    place_y = lax.axis_index("dy")

    def domain(i, j):
        return lax.rem(place_x + i + count_x, count_x), lax.rem(place_y + j + count_y, count_y)

    def owner(i, j):
        x, y = domain(i, j)
        return x * count_y + y

    def slot_of(i, j):
        return 3 * (i + 1) + j + 1

    edge = (place_x == 0) | (place_x == count_x - 1)
    near = jnp.where(place_x == 0, 1, -1)
    side = 1 - 2 * lax.rem(place_y, 2)
    order = [
        (0, 0),
        (0, side),
        (0, -side),
        (near, 0),
        (near, side),
        None,
        (near, -side),
        (-near, 0),
        (-near, side),
        (-near, -side),
    ]

    def target(i, j, along):
        x, y = domain(i, j)
        return {"dx": x} if along == "dx" else {"dy": y}

    barrier = pltpu.get_barrier_semaphore()
    for step in ((1, 0, "dx"), (-1, 0, "dx"), (0, 1, "dy"), (0, -1, "dy")):
        pl.semaphore_signal(
            barrier, inc=1, device_id=target(*step), device_id_type=pl.DeviceIdType.MESH
        )

    local = [
        pltpu.make_async_copy(src, dst, local_sem.at[k])
        for k, (src, dst) in enumerate(
            (
                (offsets_in, offsets),
                (list_in, pair_list),
                (mask_in, pair_mask),
                (own_in, own),
                (table_in, table),
            )
        )
    ]
    for copy in local:
        copy.start()
    tally[...] = jnp.zeros_like(tally)
    for copy in local[:3]:
        copy.wait()
    for row, (i, j) in enumerate(CELLS):
        number = jnp.int32(0)
        for slot in range(pair_mask.shape[0]):
            same = pair_list[1, slot] == owner(i, j)
            number = number + jnp.where(same, pair_mask[slot], 0)
        tally[row : row + 1, :] = jnp.full((1, 2 * box), 1.0, jnp.float32) * number.astype(
            jnp.float32
        )
    mine = owner(0, 0)
    for unit, cell in enumerate(order):
        other = mine if cell is None else owner(*cell)
        for axis in range(3):
            moves[unit, axis] = offsets[axis, mine] - offsets[axis, other]

    pl.semaphore_wait(barrier, 4)

    def copies(source, i, j, along, relayed=False):
        slot = slot_of(source[0] - i, source[1] - j)
        block, number = (own_in, tally)
        if relayed:
            block = landed.at[slot_of(*source)]
            number = landed_tally.at[slot_of(*source)]
        return [
            pltpu.make_async_remote_copy(
                src_ref=src,
                dst_ref=dst.at[slot],
                send_sem=send.at[slot],
                recv_sem=recv.at[slot],
                device_id=target(i, j, along),
                device_id_type=pl.DeviceIdType.MESH,
            )
            for src, dst, send, recv in (
                (block, landed, send_sem, recv_sem),
                (number, landed_tally, tally_send, tally_recv),
            )
        ]

    def start(made):
        for copy in made:
            copy.start()

    def arrived(i, j):
        slot = slot_of(i, j)
        for src, dst, send, recv in (
            (own_in, landed, send_sem, recv_sem),
            (tally, landed_tally, tally_send, tally_recv),
        ):
            pltpu.make_async_remote_copy(
                src_ref=src,
                dst_ref=dst.at[slot],
                send_sem=send.at[slot],
                recv_sem=recv.at[slot],
                device_id=target(0, 1, "dy"),
                device_id_type=pl.DeviceIdType.MESH,
            ).wait_recv()

    own_y = [copies((0, 0), 0, j, "dy") for j in (-side, side)]
    to_near = copies((0, 0), near, 0, "dx")
    to_far = copies((0, 0), -near, 0, "dx")
    relay_near = [copies((near, 0), 0, j, "dy", True) for j in (-side, side)]
    relay_far = [copies((-near, 0), 0, j, "dy", True) for j in (-side, side)]
    start(to_near)

    @pl.when(jnp.logical_not(edge))
    def _():
        start(to_far)

    for made in own_y:
        start(made)

    lane = lax.broadcasted_iota(jnp.int32, (box, 2 * box), 1)
    low_half = lane < box

    staged[...] = jnp.zeros_like(staged)
    total[...] = jnp.zeros_like(total)
    place_own = placing(box, None, 0)

    def square(index):
        freq = jnp.where(index <= box // 2, index, index - box // 2).astype(jnp.float32)
        return (2.0 * math.pi / box * freq) * (2.0 * math.pi / box * freq)

    plane = square(lax.broadcasted_iota(jnp.int32, (box, 2 * box), 0))
    plane = plane + square(jnp.where(low_half, lane, lane - box)) + (8.0 * math.pi / box) ** 2
    local[3].wait()

    def placed(j, blocks, table, write):
        parts = []
        for c in range(CHUNKS):
            here = pl.ds(pl.multiple_of((j * CHUNKS + c) * 4 * box, 4 * box), 4 * box)
            parts.append(jnp.concatenate([block[:, here] for block in blocks], axis=1))
        res = jnp.dot(jnp.concatenate(parts, axis=0), table, preferred_element_type=jnp.float32)
        for c in range(CHUNKS):
            for i in range(4):
                y = (j * CHUNKS + c) * 4 + i
                write(y, res[box * c : box * (c + 1), 2 * box * i : 2 * box * (i + 1)])

    def prepare(j, carry):
        def write(y, tile):
            begin = pl.multiple_of(y * box, box)
            phi[pl.ds(begin, box), :] = tile
            green[pl.ds(begin, box), :] = 1.0 / (plane + square(y))

        placed(j, [own], place_own, write)
        return carry

    lax.fori_loop(0, chunks // CHUNKS, prepare, 0)
    local[4].wait()
    left_f = table.at[0 : 2 * box, 0 : 2 * box]
    left_i = table.at[0 : 2 * box, 2 * box : 4 * box]
    right_f = table.at[2 * box : 6 * box, :]
    right_i = table.at[6 * box : 10 * box, :]

    def one_pair(p, carry):
        unit_a, unit_b = 2 * p, 2 * p + 1

        place = jnp.concatenate(
            [placing(box, 0, moves[unit_a, 2]), placing(box, 1, moves[unit_b, 2])], axis=0
        )
        for q in range(PAIRS):

            @pl.when(p == q)
            def _():
                blocks, rows = [], []
                for unit in (2 * q, 2 * q + 1):
                    if order[unit] is None or unit == 0:
                        row = slot_of(0, 0)
                        blocks.append(own)
                        rows.append(tally[row : row + 1, :] * (2.0 if unit == 0 else 0.0))
                        continue
                    if unit not in (3, 7):
                        arrived(*order[unit])
                    slot = slot_of(*order[unit])
                    blocks.append(landed.at[slot])
                    rows.append(
                        tally[pl.ds(slot, 1), :] + landed_tally[slot, pl.ds(8 - slot, 1), :]
                    )
                weights[...] = jnp.where(low_half[0:8], rows[0], rows[1])

                def stage(j, inner):
                    def write(y, tile):
                        start = pl.multiple_of(y * 2 * box + box // 2, box // 2)
                        staged[pl.ds(start, box), :] = tile

                    placed(j, blocks, place, write)
                    return inner

                lax.fori_loop(0, chunks // CHUNKS, stage, 0)

        def fetch(y, unit):
            source = y + moves[unit, 1]
            inside = (source >= 0) & (source < box)
            row = jnp.clip(source, 0, box - 1) * 2 * box + box // 2 + moves[unit, 0]
            return staged[pl.ds(row, box), :] * jnp.where(inside, 1.0, 0.0)

        def forward(g, inner):
            tiles = []
            for i in range(GROUP):
                y = g * GROUP + i
                start = pl.multiple_of(y * box, box)
                moved = jnp.where(low_half, fetch(y, unit_a), fetch(y, unit_b))
                partner[pl.ds(start, box), :] = moved
                tiles.append(moved * phi[pl.ds(start, box), :])
            tiles = apply_right(right_f[...], apply_left(left_f[...], tiles))
            for i in range(GROUP):
                start = pl.multiple_of((g * GROUP + i) * pitch, 8)
                work[pl.ds(start, box), :] = tiles[i]
            return inner

        lax.fori_loop(0, box // GROUP, forward, 0)

        @pl.when((p == 0) & edge)
        def _():
            start(to_far)

        @pl.when(p == 2)
        def _():
            arrived(-near, 0)
            for made in relay_far:
                start(made)

        def middle(g, inner):
            tiles = []
            for i in range(GROUP):
                tiles.append(work[pl.ds(g * GROUP + i, box, stride=pitch), :])
            tiles = apply_left(left_f[...], tiles)
            for i in range(GROUP):
                start = pl.multiple_of((g * GROUP + i) * box, box)
                tiles[i] = tiles[i] * green[pl.ds(start, box), :]
            tiles = apply_left(left_i[...], tiles)
            for i in range(GROUP):
                work[pl.ds(g * GROUP + i, box, stride=pitch), :] = tiles[i]
            return inner

        lax.fori_loop(0, box // GROUP, middle, 0)

        def back(g, inner):
            tiles = []
            for i in range(GROUP):
                start = pl.multiple_of((g * GROUP + i) * pitch, 8)
                tiles.append(work[pl.ds(start, box), :])
            tiles = apply_left(left_i[...], apply_right(right_i[...], tiles))
            weight = weights[0:1, :]
            for i in range(GROUP):
                start = pl.multiple_of((g * GROUP + i) * box, box)
                here = pl.ds(start, box)
                total[here, :] = total[here, :] + tiles[i] * partner[here, :] * weight
            return inner

        lax.fori_loop(0, box // GROUP, back, 0)

        @pl.when(p == 0)
        def _():
            arrived(near, 0)
            for made in relay_near:
                start(made)

        return carry

    lax.fori_loop(0, PAIRS, one_pair, 0)

    def finish(j, carry):
        even = total[pl.ds(pl.multiple_of(2 * j * box, box), box), :]
        odd = total[pl.ds(pl.multiple_of((2 * j + 1) * box, box), box), :]
        even = even + pltpu.roll(even, box, 1)
        odd = odd + pltpu.roll(odd, box, 1)
        here = pl.ds(pl.multiple_of(j * 2 * box, 2 * box), 2 * box)
        out[:, here] = jnp.where(low_half, even, odd)
        return carry

    lax.fori_loop(0, box // 2, finish, 0)
    for made in [to_near, to_far] + own_y + relay_near + relay_far:
        for copy in made:
            copy.wait_send()


def body(orbitals, offsets, pair_list, pair_mask):
    box, flat = orbitals.shape[1:]
    table = jnp.asarray(tables(box))
    vmem = pl.BlockSpec(memory_space=pltpu.VMEM)
    stay = pl.BlockSpec(memory_space=pl.ANY)
    rows = box * box
    macs = PAIRS * 7 * 4096 * 65536
    slots = len(CELLS)
    out = pl.pallas_call(
        functools.partial(kernel, lax.axis_size("dx"), lax.axis_size("dy"), box),
        out_shape=jax.ShapeDtypeStruct((box, flat), jnp.float32),
        in_specs=[stay] * 5,
        out_specs=vmem,
        scratch_shapes=[
            pltpu.VMEM((2 * rows, 2 * box), jnp.float32),
            pltpu.VMEM((rows, 2 * box), jnp.float32),
            pltpu.VMEM((box * (box + 8), 2 * box), jnp.float32),
            pltpu.VMEM((rows, 2 * box), jnp.float32),
            pltpu.VMEM((rows, 2 * box), jnp.float32),
            pltpu.VMEM((rows, 2 * box), jnp.float32),
            pltpu.VMEM((16, 2 * box), jnp.float32),
            pltpu.VMEM((8, 2 * box), jnp.float32),
            pltpu.SMEM((2 * PAIRS, 3), jnp.int32),
            pltpu.VMEM((slots, box, flat), jnp.bfloat16),
            pltpu.VMEM((slots, 16, 2 * box), jnp.float32),
            pltpu.SMEM(offsets.shape[::-1], jnp.int32),
            pltpu.SMEM(pair_list.shape[::-1], jnp.int32),
            pltpu.SMEM(pair_mask.shape, jnp.int32),
            pltpu.VMEM(table.shape, jnp.bfloat16),
            pltpu.VMEM((box, flat), jnp.bfloat16),
        ]
        + [pltpu.SemaphoreType.DMA((slots,))] * 4
        + [pltpu.SemaphoreType.DMA((5,))],
        compiler_params=pltpu.CompilerParams(
            vmem_limit_bytes=60 * 1024 * 1024, collective_id=0, has_side_effects=True
        ),
        cost_estimate=pl.CostEstimate(
            flops=2 * macs, bytes_accessed=10 * rows * box * 2, transcendentals=0
        ),
    )(offsets.T, pair_list.T, pair_mask, table, orbitals[0])
    return out[None]


def solution(mesh):
    placed = (P(("dx", "dy"), None, None), P(), P(("dx", "dy"), None), P(("dx", "dy")))
    return jax.shard_map(
        body, mesh=mesh, in_specs=placed, out_specs=P(("dx", "dy"), None, None), check_vma=False
    )
```

```python
import functools
import math

import jax
import jax.numpy as jnp
import ml_dtypes
import numpy as np
from jax import lax
from jax.experimental import pallas as pl
from jax.experimental.pallas import tpu as pltpu
from jax.sharding import PartitionSpec as P

GROUP = 16
LEFT = 2
RIGHT = 8
CHUNKS = 8
CELLS = [(i, j) for i in (-1, 0, 1) for j in (-1, 0, 1)]
PAIRS = 5


def basis(box):
    half = box // 2
    index = np.arange(box)
    freq = np.where(index <= half, index, index - half)
    angle = 2.0 * np.pi / box * ((freq[:, None] * index[None, :]) % box)
    rows = np.where(index[:, None] <= half, np.cos(angle), np.sin(angle))
    scale = np.where((index == 0) | (index == half), 1.0, math.sqrt(2.0)) / math.sqrt(box)
    return rows * scale[:, None], freq


def split_np(value):
    high = value.astype(ml_dtypes.bfloat16)
    low = (value - high.astype(np.float64)).astype(ml_dtypes.bfloat16)
    return high, low


def left_table(matrix):
    high, low = split_np(matrix)
    return np.concatenate([high, high, low, np.zeros_like(low)], axis=1)


def right_table(matrix):
    high, low = split_np(np.kron(np.eye(2), matrix))
    return np.block([[high, low], [high, np.zeros_like(low)]])


def tables(box):
    rows, freq = basis(box)
    lefts = np.concatenate([left_table(rows), left_table(rows.T)], axis=0)
    return np.concatenate([lefts, right_table(rows.T), right_table(rows)], axis=0)


def split(value):
    high = value.astype(jnp.bfloat16)
    low = (value - high.astype(jnp.float32)).astype(jnp.bfloat16)
    return high, low


def apply_left(table, tiles):
    box, lanes = tiles[0].shape
    made = []
    for first in range(0, len(tiles), LEFT):
        high, low = split(jnp.concatenate(tiles[first : first + LEFT], axis=1))
        terms = jnp.concatenate([high, low, high], axis=0)
        out = jnp.dot(table, terms, preferred_element_type=jnp.float32)
        made += [out[:, lanes * i : lanes * (i + 1)] for i in range(LEFT)]
    return made


def apply_right(table, tiles):
    box, lanes = tiles[0].shape
    made = []
    for first in range(0, len(tiles), RIGHT):
        high, low = split(jnp.concatenate(tiles[first : first + RIGHT], axis=0))
        both = jnp.concatenate([high, low], axis=1)
        out = jnp.dot(both, table, preferred_element_type=jnp.float32)
        out = out[:, :lanes] + out[:, lanes:]
        made += [out[box * i : box * (i + 1)] for i in range(RIGHT)]
    return made


def placing(box, which, move_z):
    rows = lax.broadcasted_iota(jnp.int32, (4 * box, 8 * box), 0)
    cols = lax.broadcasted_iota(jnp.int32, (4 * box, 8 * box), 1)
    keep = (rows // box == cols // (2 * box)) & (rows % box == cols % box + move_z)
    if which is not None:
        keep = keep & ((cols // box) % 2 == which)
    return jnp.where(keep, 1.0, 0.0).astype(jnp.bfloat16)


def kernel(count_x, count_y, box, *refs):
    offsets_in, list_in, mask_in, table_in, own_in = refs[:5]
    out, staged, partner, work, total, phi, green = refs[5:12]
    tally, weights, moves, landed, landed_tally = refs[12:17]
    offsets, pair_list, pair_mask, table, own = refs[17:22]
    send_sem, recv_sem, tally_send, tally_recv, local_sem = refs[22:]
    chunks = box // 4
    pitch = box + 8

    place_x = lax.axis_index("dx")
    place_y = lax.axis_index("dy")

    def domain(i, j):
        return lax.rem(place_x + i + count_x, count_x), lax.rem(place_y + j + count_y, count_y)

    def owner(i, j):
        x, y = domain(i, j)
        return x * count_y + y

    def slot_of(i, j):
        return 3 * (i + 1) + j + 1

    edge = (place_x == 0) | (place_x == count_x - 1)
    near = jnp.where(place_x == 0, 1, -1)
    side = 1 - 2 * lax.rem(place_y, 2)
    order = [
        (0, 0),
        (0, side),
        (0, -side),
        (near, 0),
        (near, side),
        None,
        (near, -side),
        (-near, 0),
        (-near, side),
        (-near, -side),
    ]

    def target(i, j, along):
        x, y = domain(i, j)
        return {"dx": x} if along == "dx" else {"dy": y}

    barrier = pltpu.get_barrier_semaphore()
    for step in ((1, 0, "dx"), (-1, 0, "dx"), (0, 1, "dy"), (0, -1, "dy")):
        pl.semaphore_signal(
            barrier, inc=1, device_id=target(*step), device_id_type=pl.DeviceIdType.MESH
        )

    local = [
        pltpu.make_async_copy(src, dst, local_sem.at[k])
        for k, (src, dst) in enumerate(
            (
                (offsets_in, offsets),
                (list_in, pair_list),
                (mask_in, pair_mask),
                (own_in, own),
                (table_in, table),
            )
        )
    ]
    for copy in local:
        copy.start()
    staged[...] = jnp.zeros_like(staged)
    total[...] = jnp.zeros_like(total)
    tally[...] = jnp.zeros_like(tally)
    for copy in local[:3]:
        copy.wait()
    for row, (i, j) in enumerate(CELLS):
        number = jnp.int32(0)
        for slot in range(pair_mask.shape[0]):
            same = pair_list[1, slot] == owner(i, j)
            number = number + jnp.where(same, pair_mask[slot], 0)
        tally[row : row + 1, :] = jnp.full((1, 2 * box), 1.0, jnp.float32) * number.astype(
            jnp.float32
        )
    mine = owner(0, 0)
    for unit, cell in enumerate(order):
        other = mine if cell is None else owner(*cell)
        for axis in range(3):
            moves[unit, axis] = offsets[axis, mine] - offsets[axis, other]

    pl.semaphore_wait(barrier, 4)

    def copies(source, i, j, along, relayed=False):
        slot = slot_of(source[0] - i, source[1] - j)
        block, number = (own_in, tally)
        if relayed:
            block = landed.at[slot_of(*source)]
            number = landed_tally.at[slot_of(*source)]
        return [
            pltpu.make_async_remote_copy(
                src_ref=src,
                dst_ref=dst.at[slot],
                send_sem=send.at[slot],
                recv_sem=recv.at[slot],
                device_id=target(i, j, along),
                device_id_type=pl.DeviceIdType.MESH,
            )
            for src, dst, send, recv in (
                (block, landed, send_sem, recv_sem),
                (number, landed_tally, tally_send, tally_recv),
            )
        ]

    def start(made):
        for copy in made:
            copy.start()

    def arrived(i, j):
        slot = slot_of(i, j)
        for src, dst, send, recv in (
            (own_in, landed, send_sem, recv_sem),
            (tally, landed_tally, tally_send, tally_recv),
        ):
            pltpu.make_async_remote_copy(
                src_ref=src,
                dst_ref=dst.at[slot],
                send_sem=send.at[slot],
                recv_sem=recv.at[slot],
                device_id=target(0, 1, "dy"),
                device_id_type=pl.DeviceIdType.MESH,
            ).wait_recv()

    own_y = [copies((0, 0), 0, j, "dy") for j in (-side, side)]
    to_near = copies((0, 0), near, 0, "dx")
    to_far = copies((0, 0), -near, 0, "dx")
    relay_near = [copies((near, 0), 0, j, "dy", True) for j in (-side, side)]
    relay_far = [copies((-near, 0), 0, j, "dy", True) for j in (-side, side)]
    start(to_near)

    @pl.when(jnp.logical_not(edge))
    def _():
        start(to_far)

    for made in own_y:
        start(made)

    lane = lax.broadcasted_iota(jnp.int32, (box, 2 * box), 1)
    low_half = lane < box

    place_own = placing(box, None, 0)

    def square(index):
        freq = jnp.where(index <= box // 2, index, index - box // 2).astype(jnp.float32)
        return (2.0 * math.pi / box * freq) * (2.0 * math.pi / box * freq)

    plane = square(lax.broadcasted_iota(jnp.int32, (box, 2 * box), 0))
    plane = plane + square(jnp.where(low_half, lane, lane - box)) + (8.0 * math.pi / box) ** 2
    local[3].wait()

    def placed(j, blocks, table, write):
        parts = []
        for c in range(CHUNKS):
            here = pl.ds(pl.multiple_of((j * CHUNKS + c) * 4 * box, 4 * box), 4 * box)
            parts.append(jnp.concatenate([block[:, here] for block in blocks], axis=1))
        res = jnp.dot(jnp.concatenate(parts, axis=0), table, preferred_element_type=jnp.float32)
        for c in range(CHUNKS):
            for i in range(4):
                y = (j * CHUNKS + c) * 4 + i
                write(y, res[box * c : box * (c + 1), 2 * box * i : 2 * box * (i + 1)])

    def prepare(j, carry):
        def write(y, tile):
            begin = pl.multiple_of(y * box, box)
            phi[pl.ds(begin, box), :] = tile
            green[pl.ds(begin, box), :] = 1.0 / (plane + square(y))

        placed(j, [own], place_own, write)
        return carry

    lax.fori_loop(0, chunks // CHUNKS, prepare, 0)
    local[4].wait()
    left_f = table.at[0:box, 0 : 3 * box]
    left_i = table.at[box : 2 * box, 0 : 3 * box]
    right_f = table.at[2 * box : 6 * box, :]
    right_i = table.at[6 * box : 10 * box, :]

    def one_pair(p, carry):
        unit_a, unit_b = 2 * p, 2 * p + 1

        place = jnp.concatenate(
            [placing(box, 0, moves[unit_a, 2]), placing(box, 1, moves[unit_b, 2])], axis=0
        )
        for q in range(PAIRS):

            @pl.when(p == q)
            def _():
                blocks, rows = [], []
                for unit in (2 * q, 2 * q + 1):
                    if order[unit] is None or unit == 0:
                        row = slot_of(0, 0)
                        blocks.append(own)
                        rows.append(tally[row : row + 1, :] * (2.0 if unit == 0 else 0.0))
                        continue
                    if unit not in (3, 7):
                        arrived(*order[unit])
                    slot = slot_of(*order[unit])
                    blocks.append(landed.at[slot])
                    rows.append(
                        tally[pl.ds(slot, 1), :] + landed_tally[slot, pl.ds(8 - slot, 1), :]
                    )
                weights[...] = jnp.where(low_half[0:8], rows[0], rows[1])

                def stage(j, inner):
                    def write(y, tile):
                        start = pl.multiple_of(y * 2 * box + box // 2, box // 2)
                        staged[pl.ds(start, box), :] = tile

                    placed(j, blocks, place, write)
                    return inner

                lax.fori_loop(0, chunks // CHUNKS, stage, 0)

        def fetch(y, unit):
            source = y + moves[unit, 1]
            inside = (source >= 0) & (source < box)
            row = jnp.where(inside, source, box) * 2 * box + box // 2 + moves[unit, 0]
            return staged[pl.ds(row, box), :]

        def forward(g, inner):
            tiles = []
            for i in range(GROUP):
                y = g * GROUP + i
                start = pl.multiple_of(y * box, box)
                moved = jnp.where(low_half, fetch(y, unit_a), fetch(y, unit_b))
                partner[pl.ds(start, box), :] = moved
                tiles.append(moved * phi[pl.ds(start, box), :])
            tiles = apply_right(right_f[...], apply_left(left_f[...], tiles))
            for i in range(GROUP):
                start = pl.multiple_of((g * GROUP + i) * pitch, 8)
                work[pl.ds(start, box), :] = tiles[i]
            return inner

        lax.fori_loop(0, box // GROUP, forward, 0)

        @pl.when((p == 0) & edge)
        def _():
            start(to_far)

        @pl.when(p == 2)
        def _():
            arrived(-near, 0)
            for made in relay_far:
                start(made)

        def middle(g, inner):
            tiles = []
            for i in range(GROUP):
                tiles.append(work[pl.ds(g * GROUP + i, box, stride=pitch), :])
            tiles = apply_left(left_f[...], tiles)
            for i in range(GROUP):
                start = pl.multiple_of((g * GROUP + i) * box, box)
                tiles[i] = tiles[i] * green[pl.ds(start, box), :]
            tiles = apply_left(left_i[...], tiles)
            for i in range(GROUP):
                work[pl.ds(g * GROUP + i, box, stride=pitch), :] = tiles[i]
            return inner

        lax.fori_loop(0, box // GROUP, middle, 0)

        def back(g, inner):
            tiles = []
            for i in range(GROUP):
                start = pl.multiple_of((g * GROUP + i) * pitch, 8)
                tiles.append(work[pl.ds(start, box), :])
            tiles = apply_left(left_i[...], apply_right(right_i[...], tiles))
            weight = weights[0:1, :]
            for i in range(GROUP):
                start = pl.multiple_of((g * GROUP + i) * box, box)
                here = pl.ds(start, box)
                total[here, :] = total[here, :] + tiles[i] * partner[here, :] * weight
            return inner

        lax.fori_loop(0, box // GROUP, back, 0)

        @pl.when(p == 0)
        def _():
            arrived(near, 0)
            for made in relay_near:
                start(made)

        return carry

    lax.fori_loop(0, PAIRS, one_pair, 0)

    def finish(j, carry):
        even = total[pl.ds(pl.multiple_of(2 * j * box, box), box), :]
        odd = total[pl.ds(pl.multiple_of((2 * j + 1) * box, box), box), :]
        even = even + pltpu.roll(even, box, 1)
        odd = odd + pltpu.roll(odd, box, 1)
        here = pl.ds(pl.multiple_of(j * 2 * box, 2 * box), 2 * box)
        out[:, here] = jnp.where(low_half, even, odd)
        return carry

    lax.fori_loop(0, box // 2, finish, 0)
    for made in [to_near, to_far] + own_y + relay_near + relay_far:
        for copy in made:
            copy.wait_send()


def body(orbitals, offsets, pair_list, pair_mask):
    box, flat = orbitals.shape[1:]
    table = jnp.asarray(tables(box))
    vmem = pl.BlockSpec(memory_space=pltpu.VMEM)
    stay = pl.BlockSpec(memory_space=pl.ANY)
    rows = box * box
    macs = PAIRS * 7 * 4096 * 65536
    slots = len(CELLS)
    out = pl.pallas_call(
        functools.partial(kernel, lax.axis_size("dx"), lax.axis_size("dy"), box),
        out_shape=jax.ShapeDtypeStruct((box, flat), jnp.float32),
        in_specs=[stay] * 5,
        out_specs=vmem,
        scratch_shapes=[
            pltpu.VMEM((2 * rows + 2 * box, 2 * box), jnp.float32),
            pltpu.VMEM((rows, 2 * box), jnp.float32),
            pltpu.VMEM((box * (box + 8), 2 * box), jnp.float32),
            pltpu.VMEM((rows, 2 * box), jnp.float32),
            pltpu.VMEM((rows, 2 * box), jnp.float32),
            pltpu.VMEM((rows, 2 * box), jnp.float32),
            pltpu.VMEM((16, 2 * box), jnp.float32),
            pltpu.VMEM((8, 2 * box), jnp.float32),
            pltpu.SMEM((2 * PAIRS, 3), jnp.int32),
            pltpu.VMEM((slots, box, flat), jnp.bfloat16),
            pltpu.VMEM((slots, 16, 2 * box), jnp.float32),
            pltpu.SMEM(offsets.shape[::-1], jnp.int32),
            pltpu.SMEM(pair_list.shape[::-1], jnp.int32),
            pltpu.SMEM(pair_mask.shape, jnp.int32),
            pltpu.VMEM(table.shape, jnp.bfloat16),
            pltpu.VMEM((box, flat), jnp.bfloat16),
        ]
        + [pltpu.SemaphoreType.DMA((slots,))] * 4
        + [pltpu.SemaphoreType.DMA((5,))],
        compiler_params=pltpu.CompilerParams(
            vmem_limit_bytes=60 * 1024 * 1024, collective_id=0, has_side_effects=True
        ),
        cost_estimate=pl.CostEstimate(
            flops=2 * macs, bytes_accessed=10 * rows * box * 2, transcendentals=0
        ),
    )(offsets.T, pair_list.T, pair_mask, table, orbitals[0])
    return out[None]


def solution(mesh):
    placed = (P(("dx", "dy"), None, None), P(), P(("dx", "dy"), None), P(("dx", "dy")))
    return jax.shard_map(
        body, mesh=mesh, in_specs=placed, out_specs=P(("dx", "dy"), None, None), check_vma=False
    )
```

```python
import functools
import math

import jax
import jax.numpy as jnp
import ml_dtypes
import numpy as np
from jax import lax
from jax.experimental import pallas as pl
from jax.experimental.pallas import tpu as pltpu
from jax.sharding import PartitionSpec as P

GROUP = 16
LEFT = 2
RIGHT = 8
CHUNKS = 8
CELLS = [(i, j) for i in (-1, 0, 1) for j in (-1, 0, 1)]
PAIRS = 5


def basis(box):
    half = box // 2
    index = np.arange(box)
    freq = np.where(index <= half, index, index - half)
    angle = 2.0 * np.pi / box * ((freq[:, None] * index[None, :]) % box)
    rows = np.where(index[:, None] <= half, np.cos(angle), np.sin(angle))
    scale = np.where((index == 0) | (index == half), 1.0, math.sqrt(2.0)) / math.sqrt(box)
    return rows * scale[:, None], freq


def split_np(value):
    high = value.astype(ml_dtypes.bfloat16)
    low = (value - high.astype(np.float64)).astype(ml_dtypes.bfloat16)
    return high, low


def left_table(matrix):
    high, low = split_np(matrix)
    return np.concatenate([high, high, low, np.zeros_like(low)], axis=1)


def right_table(matrix):
    high, low = split_np(np.kron(np.eye(2), matrix))
    return np.block([[high, low], [high, np.zeros_like(low)]])


def tables(box):
    rows, freq = basis(box)
    lefts = np.concatenate([left_table(rows), left_table(rows.T)], axis=0)
    return np.concatenate([lefts, right_table(rows.T), right_table(rows)], axis=0)


def split(value):
    high = value.astype(jnp.bfloat16)
    low = (value - high.astype(jnp.float32)).astype(jnp.bfloat16)
    return high, low


def apply_left(table, tiles):
    box, lanes = tiles[0].shape
    made = []
    for first in range(0, len(tiles), LEFT):
        high, low = split(jnp.concatenate(tiles[first : first + LEFT], axis=1))
        terms = jnp.concatenate([high, low, high], axis=0)
        out = jnp.dot(table, terms, preferred_element_type=jnp.float32)
        made += [out[:, lanes * i : lanes * (i + 1)] for i in range(LEFT)]
    return made


def apply_right(table, tiles):
    box, lanes = tiles[0].shape
    made = []
    for first in range(0, len(tiles), RIGHT):
        high, low = split(jnp.concatenate(tiles[first : first + RIGHT], axis=0))
        both = jnp.concatenate([high, low], axis=1)
        out = jnp.dot(both, table, preferred_element_type=jnp.float32)
        out = out[:, :lanes] + out[:, lanes:]
        made += [out[box * i : box * (i + 1)] for i in range(RIGHT)]
    return made


def placing(box, which, move_z):
    rows = lax.broadcasted_iota(jnp.int32, (4 * box, 8 * box), 0)
    cols = lax.broadcasted_iota(jnp.int32, (4 * box, 8 * box), 1)
    keep = (rows // box == cols // (2 * box)) & (rows % box == cols % box + move_z)
    if which is not None:
        keep = keep & ((cols // box) % 2 == which)
    return jnp.where(keep, 1.0, 0.0).astype(jnp.bfloat16)


def kernel(count_x, count_y, box, *refs):
    offsets_in, list_in, mask_in, table_in, own_in = refs[:5]
    out, staged, partner, work, total, phi, green = refs[5:12]
    tally, weights, moves, landed, landed_tally = refs[12:17]
    offsets, pair_list, pair_mask, table, own = refs[17:22]
    send_sem, recv_sem, tally_send, tally_recv, local_sem = refs[22:]
    chunks = box // 4
    pitch = box + 8

    place_x = lax.axis_index("dx")
    place_y = lax.axis_index("dy")

    def domain(i, j):
        return lax.rem(place_x + i + count_x, count_x), lax.rem(place_y + j + count_y, count_y)

    def owner(i, j):
        x, y = domain(i, j)
        return x * count_y + y

    def slot_of(i, j):
        return 3 * (i + 1) + j + 1

    edge = (place_x == 0) | (place_x == count_x - 1)
    near = jnp.where(place_x == 0, 1, -1)
    side = 1 - 2 * lax.rem(place_y, 2)
    order = [
        (0, 0),
        (0, side),
        (0, -side),
        (near, 0),
        (near, side),
        None,
        (near, -side),
        (-near, 0),
        (-near, side),
        (-near, -side),
    ]

    def target(i, j, along):
        x, y = domain(i, j)
        return {"dx": x} if along == "dx" else {"dy": y}

    barrier = pltpu.get_barrier_semaphore()
    for step in ((1, 0, "dx"), (-1, 0, "dx"), (0, 1, "dy"), (0, -1, "dy")):
        pl.semaphore_signal(
            barrier, inc=1, device_id=target(*step), device_id_type=pl.DeviceIdType.MESH
        )

    local = [
        pltpu.make_async_copy(src, dst, local_sem.at[k])
        for k, (src, dst) in enumerate(
            (
                (offsets_in, offsets),
                (list_in, pair_list),
                (mask_in, pair_mask),
                (own_in, own),
                (table_in, table),
            )
        )
    ]
    for copy in local:
        copy.start()
    staged[...] = jnp.zeros_like(staged)
    total[...] = jnp.zeros_like(total)
    tally[...] = jnp.zeros_like(tally)
    for copy in local[:3]:
        copy.wait()
    for row, (i, j) in enumerate(CELLS):
        number = jnp.int32(0)
        for slot in range(pair_mask.shape[0]):
            same = pair_list[1, slot] == owner(i, j)
            number = number + jnp.where(same, pair_mask[slot], 0)
        tally[row : row + 1, :] = jnp.full((1, 2 * box), 1.0, jnp.float32) * number.astype(
            jnp.float32
        )
    mine = owner(0, 0)
    for unit, cell in enumerate(order):
        other = mine if cell is None else owner(*cell)
        for axis in range(3):
            moves[unit, axis] = offsets[axis, mine] - offsets[axis, other]

    pl.semaphore_wait(barrier, 4)

    def copies(source, i, j, along, relayed=False):
        slot = slot_of(source[0] - i, source[1] - j)
        block, number = (own_in, tally)
        if relayed:
            block = landed.at[slot_of(*source)]
            number = landed_tally.at[slot_of(*source)]
        return [
            pltpu.make_async_remote_copy(
                src_ref=src,
                dst_ref=dst.at[slot],
                send_sem=send.at[slot],
                recv_sem=recv.at[slot],
                device_id=target(i, j, along),
                device_id_type=pl.DeviceIdType.MESH,
            )
            for src, dst, send, recv in (
                (block, landed, send_sem, recv_sem),
                (number, landed_tally, tally_send, tally_recv),
            )
        ]

    def start(made):
        for copy in made:
            copy.start()

    def arrived(i, j):
        slot = slot_of(i, j)
        for src, dst, send, recv in (
            (own_in, landed, send_sem, recv_sem),
            (tally, landed_tally, tally_send, tally_recv),
        ):
            pltpu.make_async_remote_copy(
                src_ref=src,
                dst_ref=dst.at[slot],
                send_sem=send.at[slot],
                recv_sem=recv.at[slot],
                device_id=target(0, 1, "dy"),
                device_id_type=pl.DeviceIdType.MESH,
            ).wait_recv()

    own_y = [copies((0, 0), 0, j, "dy") for j in (-side, side)]
    to_near = copies((0, 0), near, 0, "dx")
    to_far = copies((0, 0), -near, 0, "dx")
    relay_near = [copies((near, 0), 0, j, "dy", True) for j in (-side, side)]
    relay_far = [copies((-near, 0), 0, j, "dy", True) for j in (-side, side)]
    start(to_near)

    @pl.when(jnp.logical_not(edge))
    def _():
        start(to_far)

    for made in own_y:
        start(made)

    lane = lax.broadcasted_iota(jnp.int32, (box, 2 * box), 1)
    low_half = lane < box

    place_own = placing(box, None, 0)

    def square(index):
        freq = jnp.where(index <= box // 2, index, index - box // 2).astype(jnp.float32)
        return (2.0 * math.pi / box * freq) * (2.0 * math.pi / box * freq)

    plane = square(lax.broadcasted_iota(jnp.int32, (box, 2 * box), 0))
    plane = plane + square(jnp.where(low_half, lane, lane - box)) + (8.0 * math.pi / box) ** 2
    local[3].wait()

    def placed(j, blocks, table, write):
        parts = []
        for c in range(CHUNKS):
            here = pl.ds(pl.multiple_of((j * CHUNKS + c) * 4 * box, 4 * box), 4 * box)
            parts.append(jnp.concatenate([block[:, here] for block in blocks], axis=1))
        res = jnp.dot(jnp.concatenate(parts, axis=0), table, preferred_element_type=jnp.float32)
        for c in range(CHUNKS):
            for i in range(4):
                y = (j * CHUNKS + c) * 4 + i
                write(y, res[box * c : box * (c + 1), 2 * box * i : 2 * box * (i + 1)])

    def prepare(j, carry):
        def write(y, tile):
            begin = pl.multiple_of(y * box, box)
            phi[pl.ds(begin, box), :] = tile
            green[pl.ds(begin, box), :] = 1.0 / (plane + square(y))

        placed(j, [own], place_own, write)
        return carry

    lax.fori_loop(0, chunks // CHUNKS, prepare, 0)

    @pl.when(edge)
    def _():
        start(to_far)

    local[4].wait()
    left_f = table.at[0:box, 0 : 3 * box]
    left_i = table.at[box : 2 * box, 0 : 3 * box]
    right_f = table.at[2 * box : 6 * box, :]
    right_i = table.at[6 * box : 10 * box, :]

    def one_pair(p, carry):
        unit_a, unit_b = 2 * p, 2 * p + 1

        place = jnp.concatenate(
            [placing(box, 0, moves[unit_a, 2]), placing(box, 1, moves[unit_b, 2])], axis=0
        )
        for q in range(PAIRS):

            @pl.when(p == q)
            def _():
                blocks, rows = [], []
                for unit in (2 * q, 2 * q + 1):
                    if order[unit] is None or unit == 0:
                        row = slot_of(0, 0)
                        blocks.append(own)
                        rows.append(tally[row : row + 1, :] * (2.0 if unit == 0 else 0.0))
                        continue
                    if unit not in (3, 7):
                        arrived(*order[unit])
                    slot = slot_of(*order[unit])
                    blocks.append(landed.at[slot])
                    rows.append(
                        tally[pl.ds(slot, 1), :] + landed_tally[slot, pl.ds(8 - slot, 1), :]
                    )
                weights[...] = jnp.where(low_half[0:8], rows[0], rows[1])

                def stage(j, inner):
                    def write(y, tile):
                        start = pl.multiple_of(y * 2 * box + box // 2, box // 2)
                        staged[pl.ds(start, box), :] = tile

                    placed(j, blocks, place, write)
                    return inner

                lax.fori_loop(0, chunks // CHUNKS, stage, 0)

        def fetch(y, unit):
            source = y + moves[unit, 1]
            inside = (source >= 0) & (source < box)
            row = jnp.where(inside, source, box) * 2 * box + box // 2 + moves[unit, 0]
            return staged[pl.ds(row, box), :]

        def forward(g, inner):
            tiles = []
            for i in range(GROUP):
                y = g * GROUP + i
                start = pl.multiple_of(y * box, box)
                moved = jnp.where(low_half, fetch(y, unit_a), fetch(y, unit_b))
                partner[pl.ds(start, box), :] = moved
                tiles.append(moved * phi[pl.ds(start, box), :])
            tiles = apply_right(right_f[...], apply_left(left_f[...], tiles))
            for i in range(GROUP):
                start = pl.multiple_of((g * GROUP + i) * pitch, 8)
                work[pl.ds(start, box), :] = tiles[i]
            return inner

        lax.fori_loop(0, box // GROUP, forward, 0)

        @pl.when(p == 2)
        def _():
            arrived(-near, 0)
            for made in relay_far:
                start(made)

        def middle(g, inner):
            tiles = []
            for i in range(GROUP):
                tiles.append(work[pl.ds(g * GROUP + i, box, stride=pitch), :])
            tiles = apply_left(left_f[...], tiles)
            for i in range(GROUP):
                start = pl.multiple_of((g * GROUP + i) * box, box)
                tiles[i] = tiles[i] * green[pl.ds(start, box), :]
            tiles = apply_left(left_i[...], tiles)
            for i in range(GROUP):
                work[pl.ds(g * GROUP + i, box, stride=pitch), :] = tiles[i]
            return inner

        lax.fori_loop(0, box // GROUP, middle, 0)

        def back(g, inner):
            tiles = []
            for i in range(GROUP):
                start = pl.multiple_of((g * GROUP + i) * pitch, 8)
                tiles.append(work[pl.ds(start, box), :])
            tiles = apply_left(left_i[...], apply_right(right_i[...], tiles))
            weight = weights[0:1, :]
            for i in range(GROUP):
                start = pl.multiple_of((g * GROUP + i) * box, box)
                here = pl.ds(start, box)
                total[here, :] = total[here, :] + tiles[i] * partner[here, :] * weight
            return inner

        lax.fori_loop(0, box // GROUP, back, 0)

        @pl.when(p == 0)
        def _():
            arrived(near, 0)
            for made in relay_near:
                start(made)

        return carry

    lax.fori_loop(0, PAIRS, one_pair, 0)

    def finish(j, carry):
        even = total[pl.ds(pl.multiple_of(2 * j * box, box), box), :]
        odd = total[pl.ds(pl.multiple_of((2 * j + 1) * box, box), box), :]
        even = even + pltpu.roll(even, box, 1)
        odd = odd + pltpu.roll(odd, box, 1)
        here = pl.ds(pl.multiple_of(j * 2 * box, 2 * box), 2 * box)
        out[:, here] = jnp.where(low_half, even, odd)
        return carry

    lax.fori_loop(0, box // 2, finish, 0)
    for made in [to_near, to_far] + own_y + relay_near + relay_far:
        for copy in made:
            copy.wait_send()


def body(orbitals, offsets, pair_list, pair_mask):
    box, flat = orbitals.shape[1:]
    table = jnp.asarray(tables(box))
    vmem = pl.BlockSpec(memory_space=pltpu.VMEM)
    stay = pl.BlockSpec(memory_space=pl.ANY)
    rows = box * box
    macs = PAIRS * 7 * 4096 * 65536
    slots = len(CELLS)
    out = pl.pallas_call(
        functools.partial(kernel, lax.axis_size("dx"), lax.axis_size("dy"), box),
        out_shape=jax.ShapeDtypeStruct((box, flat), jnp.float32),
        in_specs=[stay] * 5,
        out_specs=vmem,
        scratch_shapes=[
            pltpu.VMEM((2 * rows + 2 * box, 2 * box), jnp.float32),
            pltpu.VMEM((rows, 2 * box), jnp.float32),
            pltpu.VMEM((box * (box + 8), 2 * box), jnp.float32),
            pltpu.VMEM((rows, 2 * box), jnp.float32),
            pltpu.VMEM((rows, 2 * box), jnp.float32),
            pltpu.VMEM((rows, 2 * box), jnp.float32),
            pltpu.VMEM((16, 2 * box), jnp.float32),
            pltpu.VMEM((8, 2 * box), jnp.float32),
            pltpu.SMEM((2 * PAIRS, 3), jnp.int32),
            pltpu.VMEM((slots, box, flat), jnp.bfloat16),
            pltpu.VMEM((slots, 16, 2 * box), jnp.float32),
            pltpu.SMEM(offsets.shape[::-1], jnp.int32),
            pltpu.SMEM(pair_list.shape[::-1], jnp.int32),
            pltpu.SMEM(pair_mask.shape, jnp.int32),
            pltpu.VMEM(table.shape, jnp.bfloat16),
            pltpu.VMEM((box, flat), jnp.bfloat16),
        ]
        + [pltpu.SemaphoreType.DMA((slots,))] * 4
        + [pltpu.SemaphoreType.DMA((5,))],
        compiler_params=pltpu.CompilerParams(
            vmem_limit_bytes=60 * 1024 * 1024, collective_id=0, has_side_effects=True
        ),
        cost_estimate=pl.CostEstimate(
            flops=2 * macs, bytes_accessed=10 * rows * box * 2, transcendentals=0
        ),
    )(offsets.T, pair_list.T, pair_mask, table, orbitals[0])
    return out[None]


def solution(mesh):
    placed = (P(("dx", "dy"), None, None), P(), P(("dx", "dy"), None), P(("dx", "dy")))
    return jax.shard_map(
        body, mesh=mesh, in_specs=placed, out_specs=P(("dx", "dy"), None, None), check_vma=False
    )
```
